128 devices in a mesh: dp: 16 (over z, y_lo, core), tensor: 8 (over x, y_hi).
Axes of the slice: x: 4, y: 4 (y_hi: 2, y_lo: 2; y = y_hi * 2 + y_lo), z: 4, core: 2. Of those that a mesh axis runs over, the one named last changes fastest.
Arguments:
- attention: bfloat16 [8192, 4096], P('dp', 'tensor'), may hold values from -6 to 6
- code_blocks: bfloat16 [4096, 4096], P('tensor'), may hold values from -4 to 4
- block_scales: float32 [32, 32], P('tensor'), may hold values from 0.008 to 0.032
- residual: bfloat16 [8192, 4096], P('dp', 'tensor'), may hold values from -6 to 6
- low_feature: bfloat16 [8192, 4096], P('dp', 'tensor'), may hold values from -6 to 6
- mid_feature: bfloat16 [8192, 4096], P('dp', 'tensor'), may hold values from -6 to 6
- join_weight: bfloat16 [4096, 3, 4096], P('dp', None, 'tensor'), may hold values from -0.0546875 to 0.0546875
- draft_gain: float32 [3, 4096], replicated, may hold values from 0.5 to 2
- cotangent: bfloat16 [3, 8192, 4096], P(None, ('dp', 'tensor')), may hold values from -24 to 24
- loss_mask: int32 [8192], P(('dp', 'tensor')), may hold values 0 or 1
Outputs:
- grad_join: float32 [4096, 3, 4096], P('dp', None, 'tensor')
- grad_gain: float32 [3, 4096], replicated
The draws below stay inside these ranges and needn't reach their ends.
All inputs are finite; a program needn't handle non-finite values. No bound on the sum of `loss_mask` on one device may be relied on, other than what follows from the above.
Results may differ from the reference program's by a relative error of at most 0.023.
Values may be sent and summed in bfloat16 or wider, within the bound.
No kernel may reach another device: no remote copies, remote signals or barrier semaphores. Data moves between devices by JAX's collectives and lax.ppermute only.
A program may use at most 128 MiB of HBM per device.

```python
import math
import jax
import jax.numpy as jnp
from jax import lax

D = 4096
ATTN_W = 4096
BLOCK = 128
STEPS = 3
TOK_DEV = 512
TOKENS = 8192
N_DP = 16
N_TENSOR = 8


def place_ends(entries, own_key, least, largest):
    index_at = [jax.random.randint(jax.random.fold_in(own_key, axis), (), 0, length) for axis, length in enumerate(entries.shape)]
    widest = entries.shape.index(max(entries.shape))
    neighbour = index_at[:widest] + [(index_at[widest] + 1) % entries.shape[widest]] + index_at[widest + 1:]
    return entries.at[tuple(index_at)].set(least).at[tuple(neighbour)].set(largest)


def spiked(entries, own_key, source, target, blocks, factor):
    def block_of(position):
        return (jnp.arange(entries.shape[position]) // (entries.shape[position] // blocks)).reshape((-1,) + (1,) * (entries.ndim - 1 - position))

    first = jax.random.permutation(own_key, blocks)[block_of(target)]
    other_side = (block_of(target) + blocks // 2) % blocks
    return jnp.where((block_of(source) == first) | (block_of(source) == other_side), factor * entries, entries)


def shard_levels(key, extent, pieces, smallest, largest):
    level, own = 1.0, jax.random.fold_in(key, 6)
    for position, blocks in pieces:
        draws = jnp.exp(jax.random.uniform(jax.random.fold_in(own, position), (blocks,), jnp.float32, smallest / len(pieces), largest / len(pieces)))
        level = level * jnp.repeat(draws, extent[position] // blocks).reshape([-1 if axis == position else 1 for axis in range(len(extent))])
    return level


def noise(rng, shape, scale, limit, cuts=(), dtype=jnp.bfloat16):
    entries = jax.random.normal(rng, shape, jnp.float32) * scale
    if len(cuts) > 0:
        entries = shard_levels(rng, shape, cuts, -0.22, 0.18) * entries
    return jnp.clip(entries, min=-limit, max=limit).astype(dtype)


def heavy_noise(stream_key, extent, scale, limit, cuts, heavy, kind=jnp.bfloat16):
    entries = scale * jax.random.normal(stream_key, extent, jnp.float32)
    if cuts:
        entries = entries * shard_levels(stream_key, extent, cuts, -0.22, 0.18)
    return jnp.clip(spiked(entries, jax.random.fold_in(stream_key, 3), *heavy), -limit, limit).astype(kind)


def setup_inputs(seed: int = 0) -> dict:
    streams_of = jax.random.split(jax.random.key(seed), 11)
    return {
        "attention": noise(streams_of[0], (TOKENS, ATTN_W), 1.0, 6.0, ((0, 16), (1, 8))),
        "code_blocks": noise(streams_of[1], (ATTN_W, D), 1.0, 4.0, ((0, 8),)),
        "block_scales": jnp.clip(jnp.exp(math.log(0.032) - 1.3862944 * jax.random.uniform(streams_of[2], (ATTN_W // BLOCK, D // BLOCK), jnp.float32) ** shard_levels(streams_of[2], (ATTN_W // BLOCK, D // BLOCK), ((0, 8),), -0.2, 0.2)), 0.008, 0.032),
        "residual": noise(streams_of[3], (TOKENS, D), 1.0, 6.0, ((0, 16), (1, 8))),
        "low_feature": noise(streams_of[4], (TOKENS, D), 1.0, 6.0, ((0, 16), (1, 8))),
        "mid_feature": noise(streams_of[5], (TOKENS, D), 1.0, 6.0, ((0, 16), (1, 8))),
        "join_weight": noise(streams_of[6], (D, 3, D), (3 * D) ** -0.5, 0.0546875, ((0, 16), (2, 8))),
        "draft_gain": jnp.clip(jnp.exp(jax.random.uniform(streams_of[7], (STEPS, D), jnp.float32, math.log(0.5), math.log(2.0))), 0.5, 2.0),
        "cotangent": heavy_noise(streams_of[8], (STEPS, TOKENS, D), 1.0, 24.0, ((1, 128),), (1, 2, 128, 5.5)),
        "loss_mask": place_ends((jax.random.randint(streams_of[9], (TOKENS,), 0, 4) < 3).astype(jnp.int32), jax.random.fold_in(streams_of[9], 1), 0, 1),
    }


EPS = 1e-05

def project_heads(attention, code_blocks, block_scales):
    summed = jnp.zeros((attention.shape[0], code_blocks.shape[1]), jnp.float32)
    for block_index in range(attention.shape[1] // BLOCK):
        lower = block_index * BLOCK
        product = jnp.dot(attention[:, lower:lower + BLOCK], code_blocks[lower:lower + BLOCK], preferred_element_type=jnp.float32)
        summed = summed + product * jnp.repeat(block_scales[block_index], BLOCK)[None, :]
    return summed

def draft_loss(joined_sum, gain_table, cotangent, token_mask, loss_scale):
    current = joined_sum
    running = jnp.zeros((), jnp.float32)
    keeper = token_mask.astype(jnp.float32)[:, None]
    for step_index in range(STEPS):
        square_mean = lax.optimization_barrier(jnp.mean(current * current, axis=-1, keepdims=True))
        normed = current * lax.rsqrt(square_mean + EPS) * gain_table[step_index][None, :]
        current = current + jax.nn.silu(normed)
        running = running + jnp.sum(keeper * cotangent[step_index].astype(jnp.float32) * current)
    return running * loss_scale

def rounded(value):
    return lax.optimization_barrier(value.astype(jnp.bfloat16)).astype(jnp.float32)

def reference(attention, code_blocks, block_scales, residual, low_feature, mid_feature, join_weight, draft_gain, cotangent, loss_mask):
    head_rows = ATTN_W // N_TENSOR
    columns = D // N_TENSOR
    projected = jnp.zeros((TOKENS, D), jnp.float32)
    for shard in range(N_TENSOR):
        lower = shard * head_rows
        partial_value = project_heads(attention[:, lower:lower + head_rows], code_blocks[lower:lower + head_rows], block_scales[lower // BLOCK:(lower + head_rows) // BLOCK])
        projected = projected + rounded(partial_value)
    high_feature = (residual.astype(jnp.float32) + projected).astype(jnp.bfloat16)
    joined_sum = jnp.zeros((TOKENS, D), jnp.float32)
    for shard in range(N_TENSOR):
        lower = shard * columns
        features = jnp.concatenate([low_feature[:, lower:lower + columns], mid_feature[:, lower:lower + columns], high_feature[:, lower:lower + columns]], axis=1)
        weights = join_weight[:, :, lower:lower + columns].reshape(D, 3 * columns)
        partial_value = jnp.dot(features, weights.T, preferred_element_type=jnp.float32)
        joined_sum = joined_sum + rounded(partial_value)
    loss_scale = float(TOKENS) ** (-0.5)
    joined_grad, grad_gain = jax.grad(draft_loss, argnums=(0, 1))(joined_sum, draft_gain, cotangent, loss_mask, loss_scale)
    joined_grad = joined_grad.astype(jnp.bfloat16)
    grad_join = jnp.zeros((D, 3, D), jnp.float32)
    for shard in range(N_DP):
        lower = shard * TOK_DEV
        features = jnp.concatenate([low_feature[lower:lower + TOK_DEV], mid_feature[lower:lower + TOK_DEV], high_feature[lower:lower + TOK_DEV]], axis=1)
        grad_block = jnp.dot(joined_grad[lower:lower + TOK_DEV].T, features, preferred_element_type=jnp.float32)
        grad_join = grad_join + rounded(grad_block).reshape(D, 3, D)
    return (grad_join, grad_gain)
```

```python
import jax
import jax.numpy as jnp
from jax import lax
from jax.sharding import PartitionSpec as P

BLOCK = 128
STEPS = 3
EPS = 1e-05
BF16 = jnp.bfloat16
F32 = jnp.float32


def send_x(value, hops):
    pairs = [(x * 2 + y, ((x + hops) % 4) * 2 + y) for x in range(4) for y in range(2)]
    return lax.ppermute(value, "tensor", pairs)


def send_y(value):
    return lax.ppermute(value, "tensor", [(t, t ^ 1) for t in range(8)])


def send_z(value, hops):
    return lax.ppermute(value, "dp", [(d, (d + 4 * hops) % 16) for d in range(16)])


def send_pair(value):
    return lax.ppermute(value, "dp", [(d, d ^ 2) for d in range(16)])


def send_core(value):
    return lax.ppermute(value, "dp", [(d, d ^ 1) for d in range(16)])


def draft_loss(joined_sum, gain_table, cotangent, token_mask, loss_scale):
    current = joined_sum
    running = jnp.zeros((), F32)
    keeper = token_mask.astype(F32)[:, None]
    for step_index in range(STEPS):
        square_mean = jnp.mean(current * current, axis=-1, keepdims=True)
        normed = current * lax.rsqrt(square_mean + EPS) * gain_table[step_index][None, :]
        current = current + jax.nn.silu(normed)
        running = running + jnp.sum(keeper * cotangent[step_index].astype(F32) * current)
    return running * loss_scale


def matmul(left, right, contract):
    return lax.dot_general(left, right, ((contract[:1], contract[1:]), ((), ())), preferred_element_type=F32)


def on_device(
    attention,
    code_blocks,
    block_scales,
    residual,
    low_feature,
    mid_feature,
    join_weight,
    draft_gain,
    cotangent,
    loss_mask,
):
    dp_index, tensor_index = lax.axis_index("dp"), lax.axis_index("tensor")
    z, q = dp_index // 4, dp_index % 4
    x, y = tensor_index // 2, tensor_index % 2
    tokens, width = residual.shape
    part = tokens // 8
    outs = join_weight.shape[0]

    def relative(dx, dy):
        return ((x + dx) % 4) * 2 + (y ^ dy)

    def relative_rows(value):
        return jnp.concatenate(
            [lax.dynamic_slice_in_dim(value, relative(dx, dy) * part, part, 0) for dx in range(4) for dy in range(2)], 0
        )

    scales = jnp.repeat(block_scales, BLOCK, axis=0)
    partial = {}
    for dx in (2, 1, 3, 0):
        columns = []
        for dy in range(2):
            target = relative(dx, dy)
            codes = lax.dynamic_slice_in_dim(code_blocks, target * width, width, 1)
            factor = lax.dynamic_slice_in_dim(scales, target * (width // BLOCK), width // BLOCK, 1)
            columns.append((codes.astype(F32) * jnp.repeat(factor, BLOCK, axis=1)).astype(BF16))
        partial[dx] = matmul(attention, jnp.concatenate(columns, 1), (1, 0)).astype(BF16)
    half = tokens // 2
    arrived = [send_x(partial[dx][:half], dx) for dx in (2, 1, 3)]
    crossed = send_y(jnp.stack([partial[dx][half:, width:] for dx in range(4)]))
    first = partial[0][:half].astype(F32) + sum(a.astype(F32) for a in arrived)
    second = {dx: partial[dx][half:, :width].astype(F32) + crossed[dx].astype(F32) for dx in range(4)}
    first_other = send_y(first[:, width:].astype(BF16))
    second_other = [send_x(second[dx].astype(BF16), dx) for dx in (2, 1, 3)]
    residual = residual.astype(F32)
    high_first = residual[:half] + (first[:, :width] + first_other.astype(F32))
    high_second = residual[half:] + (second[0] + sum(a.astype(F32) for a in second_other))
    high = relative_rows(jnp.concatenate([high_first.astype(BF16), high_second.astype(BF16)], 0))

    weight = jnp.transpose(join_weight, (1, 0, 2))
    weight_pair = send_pair(weight)
    weight_all = jnp.concatenate([weight, send_core(weight), weight_pair, send_core(weight_pair)], 1)
    low_mid = jnp.concatenate([relative_rows(low_feature), relative_rows(mid_feature)], 1)
    low_mids = [low_mid] + [send_z(low_mid, -dz) for dz in (1, 2, 3)]
    weight_low_mid = jnp.concatenate([weight_all[0], weight_all[1]], 1)
    early = [matmul(value, weight_low_mid, (1, 1)) for value in low_mids]

    highs = [high] + [send_z(high, -dz) for dz in (1, 2, 3)]
    joined = [(early[dz] + matmul(highs[dz], weight_all[2], (1, 1))).astype(BF16) for dz in range(4)]
    joined = [value.reshape(4, 2, part, -1) for value in joined]

    near = jnp.stack(joined[:2])
    far = jnp.stack(joined[2:])
    near_crossed = send_y(near[:, :, 1])
    far_arrived = [send_x(far[:, dx], dx) for dx in (2, 1, 3)]
    near_sum = near[:, :, 0].astype(F32) + near_crossed.astype(F32)
    far_sum = far[:, 0].astype(F32) + sum(a.astype(F32) for a in far_arrived)
    near_other = [send_x(near_sum[:, dx].astype(BF16), dx) for dx in (2, 1, 3)]
    far_other = send_y(far_sum[:, 1].astype(BF16))
    near_total = near_sum[:, 0] + sum(a.astype(F32) for a in near_other)
    far_total = far_sum[:, 0] + far_other.astype(F32)
    totals = [near_total[0]] + [
        send_z(value.astype(BF16), dz).astype(F32)
        for dz, value in ((1, near_total[1]), (2, far_total[0]), (3, far_total[1]))
    ]
    joined_sum = jnp.concatenate(totals, 1)

    def relative_features(value):
        blocks = [((z - dz) % 4) * 4 + (q ^ dq) for dz in range(4) for dq in range(4)]
        return jnp.concatenate([lax.dynamic_slice_in_dim(value, b * outs, outs, value.ndim - 1) for b in blocks], -1)

    loss_scale = float(tokens * lax.axis_size("dp")) ** (-0.5)
    joined_grad, gain_grad = jax.grad(draft_loss, argnums=(0, 1))(
        joined_sum, relative_features(draft_gain), relative_features(cotangent), loss_mask, loss_scale
    )
    absolute = [((z - b // 4) % 4) * 4 + (q ^ (b % 4)) for b in range(16)]
    gain_full = jnp.zeros_like(gain_grad)
    for b in range(16):
        gain_full = lax.dynamic_update_slice_in_dim(gain_full, gain_grad[:, b * outs : (b + 1) * outs], absolute[b] * outs, 1)
    grad_gain = gain_full
    for axis, bits in (("dp", (1, 2, 4, 8)), ("tensor", (1, 2, 4))):
        for bit in bits:
            grad_gain = grad_gain + lax.ppermute(grad_gain, axis, [(d, d ^ bit) for d in range(lax.axis_size(axis))])

    joined_grad = joined_grad.astype(BF16)
    row = 4 * outs
    grads = [joined_grad[:, :row]] + [send_z(joined_grad[:, dz * row : (dz + 1) * row], -dz) for dz in (1, 2, 3)]

    near = jnp.concatenate(grads[:2], 0)
    far = jnp.concatenate(grads[2:], 0)
    near_x = jnp.stack([near] + [send_x(near, -dx) for dx in (1, 2, 3)])
    near_all = jnp.stack([near_x, send_y(near_x)]).reshape(-1, row)
    far_y = jnp.stack([far, send_y(far)])
    far_all = jnp.stack([far_y] + [send_x(far_y, -dx) for dx in (1, 2, 3)]).reshape(-1, row)

    features = [jnp.concatenate([low_mids[dz], highs[dz]], 1).reshape(4, 2, part, -1) for dz in range(4)]
    near_features = jnp.stack(features[:2]).transpose(2, 1, 0, 3, 4).reshape(2 * tokens, -1)
    far_features = jnp.stack(features[2:]).transpose(1, 2, 0, 3, 4).reshape(2 * tokens, -1)

    def grad_block(dq):
        columns = slice(dq * outs, (dq + 1) * outs)
        return matmul(near_all[:, columns], near_features, (0, 0)) + matmul(far_all[:, columns], far_features, (0, 0))

    block3 = send_core(grad_block(3).astype(BF16))
    for_pair = send_pair((grad_block(2).astype(BF16).astype(F32) + block3.astype(F32)).astype(BF16))
    block1 = send_core(grad_block(1).astype(BF16))
    own = grad_block(0).astype(BF16).astype(F32) + block1.astype(F32)
    grad_join = (own + for_pair.astype(F32)).reshape(outs, 3, width)
    return (grad_join, grad_gain)


def solution(mesh):
    return jax.shard_map(
        on_device,
        mesh=mesh,
        in_specs=(
            P("dp", "tensor"),
            P("tensor", None),
            P("tensor", None),
            P("dp", "tensor"),
            P("dp", "tensor"),
            P("dp", "tensor"),
            P("dp", None, "tensor"),
            P(),
            P(None, ("dp", "tensor"), None),
            P(("dp", "tensor")),
        ),
        out_specs=(P("dp", None, "tensor"), P()),
        check_vma=False,
    )
```

```python
import jax
import jax.numpy as jnp
from jax import lax
from jax.experimental import pallas as pl
from jax.experimental.pallas import tpu as pltpu
from jax.sharding import PartitionSpec as P

BLOCK = 128
STEPS = 3
EPS = 1e-05
BF16 = jnp.bfloat16
F32 = jnp.float32


def send_x(value, hops):
    pairs = [(x * 2 + y, ((x + hops) % 4) * 2 + y) for x in range(4) for y in range(2)]
    return lax.ppermute(value, "tensor", pairs)


def send_y(value):
    return lax.ppermute(value, "tensor", [(t, t ^ 1) for t in range(8)])


def send_z(value, hops):
    return lax.ppermute(value, "dp", [(d, (d + 4 * hops) % 16) for d in range(16)])


def send_pair(value):
    return lax.ppermute(value, "dp", [(d, d ^ 2) for d in range(16)])


def send_core(value):
    return lax.ppermute(value, "dp", [(d, d ^ 1) for d in range(16)])


def draft_loss(joined_sum, gain_table, cotangent, token_mask, loss_scale):
    current = joined_sum
    running = jnp.zeros((), F32)
    keeper = token_mask.astype(F32)[:, None]
    for step_index in range(STEPS):
        square_mean = jnp.mean(current * current, axis=-1, keepdims=True)
        normed = current * lax.rsqrt(square_mean + EPS) * gain_table[step_index][None, :]
        current = current + jax.nn.silu(normed)
        running = running + jnp.sum(keeper * cotangent[step_index].astype(F32) * current)
    return running * loss_scale


def project_kernel(groups, places_ref, attention_ref, codes_ref, scales_ref, *out_refs):
    step = pl.program_id(0)
    place = places_ref[step]
    rows, width = attention_ref.shape[0], codes_ref.shape[1]
    blocks = width // BLOCK
    columns = [jnp.zeros((rows, BLOCK), F32) for _ in range(blocks)]
    for k in range(codes_ref.shape[0] // BLOCK):
        span = slice(k * BLOCK, (k + 1) * BLOCK)
        product = jnp.dot(attention_ref[:, span], codes_ref[span, :], preferred_element_type=F32)
        for j in range(blocks):
            columns[j] += product[:, j * BLOCK : (j + 1) * BLOCK] * scales_ref[k, place * blocks + j]
    for index, group in enumerate(groups):
        first = sum(groups[:index])

        @pl.when((step >= first) & (step < first + group))
        def _(out_ref=out_refs[index]):
            for j in range(blocks):
                out_ref[:, j * BLOCK : (j + 1) * BLOCK] = columns[j].astype(BF16)


def project(attention, code_blocks, block_scales, places, groups, width):
    rows, depth = attention.shape
    starts = [sum(groups[:i]) for i in range(len(groups))]

    def out_map(first, group):
        return lambda step, places: (jnp.clip(step - first, 0, group - 1), 0, 0)

    return pl.pallas_call(
        lambda *refs: project_kernel(groups, *refs),
        grid_spec=pltpu.PrefetchScalarGridSpec(
            num_scalar_prefetch=1,
            grid=(sum(groups),),
            in_specs=[
                pl.BlockSpec((rows, depth), lambda step, places: (0, 0)),
                pl.BlockSpec((depth, width), lambda step, places: (0, places[step])),
                pl.BlockSpec(memory_space=pltpu.SMEM),
            ],
            out_specs=[pl.BlockSpec((None, rows, width), out_map(f, g)) for f, g in zip(starts, groups)],
        ),
        out_shape=[jax.ShapeDtypeStruct((g, rows, width), BF16) for g in groups],
        compiler_params=pltpu.CompilerParams(vmem_limit_bytes=24 * 2**20),
        cost_estimate=pl.CostEstimate(
            flops=2 * rows * depth * width * sum(groups), bytes_accessed=4 * depth * width * sum(groups), transcendentals=0
        ),
    )(places, attention, code_blocks, block_scales)


def matmul(left, right, contract):
    return lax.dot_general(left, right, ((contract[:1], contract[1:]), ((), ())), preferred_element_type=F32)


def on_device(
    attention,
    code_blocks,
    block_scales,
    residual,
    low_feature,
    mid_feature,
    join_weight,
    draft_gain,
    cotangent,
    loss_mask,
):
    dp_index, tensor_index = lax.axis_index("dp"), lax.axis_index("tensor")
    z, q = dp_index // 4, dp_index % 4
    x, y = tensor_index // 2, tensor_index % 2
    tokens, width = residual.shape
    part = tokens // 8
    outs = join_weight.shape[0]

    def relative(dx, dy):
        return ((x + dx) % 4) * 2 + (y ^ dy)

    def relative_rows(value):
        return jnp.concatenate(
            [lax.dynamic_slice_in_dim(value, relative(dx, dy) * part, part, 0) for dx in range(4) for dy in range(2)], 0
        )

    z_groups = [[4 * i + j for i in range(4)] for j in range(4)]
    q_groups = [[4 * i + j for j in range(4)] for i in range(4)]
    low_mid = jnp.concatenate([relative_rows(low_feature), relative_rows(mid_feature)], 1)
    low_mid_all = lax.all_gather(low_mid, "dp", axis_index_groups=z_groups)
    weight = jnp.transpose(join_weight, (1, 0, 2))
    weight_all = lax.all_gather(weight, "dp", axis_index_groups=q_groups)

    half = tokens // 2
    second_places = jnp.stack([relative(dx, dy) for dy in (1, 0) for dx in range(4)])
    to_cross, second_own = project(attention[half:], code_blocks, block_scales, second_places, (4, 4), width)
    crossed = send_y(to_cross)
    first_places = jnp.stack([relative(dx, dy) for dx in (2, 1, 3, 0) for dy in range(2)])
    *to_send, first_own = project(attention[:half], code_blocks, block_scales, first_places, (2, 2, 2, 2), width)
    arrived = [send_x(value, dx) for dx, value in zip((2, 1, 3), to_send)]
    first = first_own.astype(F32) + sum(a.astype(F32) for a in arrived)
    second = second_own.astype(F32) + crossed.astype(F32)
    first_other = send_y(first[1].astype(BF16))
    second_other = [send_x(second[dx].astype(BF16), dx) for dx in (2, 1, 3)]
    residual = residual.astype(F32)
    high_first = residual[:half] + (first[0] + first_other.astype(F32))
    high_second = residual[half:] + (second[0] + sum(a.astype(F32) for a in second_other))
    high = relative_rows(jnp.concatenate([high_first.astype(BF16), high_second.astype(BF16)], 0))

    low_mids = [lax.dynamic_index_in_dim(low_mid_all, (z + dz) % 4, 0, False) for dz in range(4)]
    weight_all = jnp.transpose(weight_all, (1, 0, 2, 3)).reshape(3, 4 * outs, width)
    weight_low_mid = jnp.concatenate([weight_all[0], weight_all[1]], 1)
    early = [matmul(value, weight_low_mid, (1, 1)) for value in low_mids]

    highs = [high] + [send_z(high, -dz) for dz in (1, 2, 3)]
    joined = [(early[dz] + matmul(highs[dz], weight_all[2], (1, 1))).astype(BF16) for dz in range(4)]
    joined = [value.reshape(4, 2, part, -1) for value in joined]

    near = jnp.stack(joined[:2])
    far = jnp.stack(joined[2:])
    near_crossed = send_y(near[:, :, 1])
    far_arrived = [send_x(far[:, dx], dx) for dx in (2, 1, 3)]
    near_sum = near[:, :, 0].astype(F32) + near_crossed.astype(F32)
    far_sum = far[:, 0].astype(F32) + sum(a.astype(F32) for a in far_arrived)
    near_other = [send_x(near_sum[:, dx].astype(BF16), dx) for dx in (2, 1, 3)]
    far_other = send_y(far_sum[:, 1].astype(BF16))
    near_total = near_sum[:, 0] + sum(a.astype(F32) for a in near_other)
    far_total = far_sum[:, 0] + far_other.astype(F32)
    totals = [near_total[0]] + [
        send_z(value.astype(BF16), dz).astype(F32)
        for dz, value in ((1, near_total[1]), (2, far_total[0]), (3, far_total[1]))
    ]
    joined_sum = jnp.concatenate(totals, 1)

    row = 4 * outs

    def relative_features(value):
        blocks = [lax.dynamic_slice_in_dim(value, (z - dz) % 4 * row, row, value.ndim - 1) for dz in range(4)]
        return jnp.concatenate(blocks, -1)

    loss_scale = float(tokens * lax.axis_size("dp")) ** (-0.5)
    joined_grad, gain_grad = jax.grad(draft_loss, argnums=(0, 1))(
        joined_sum, relative_features(draft_gain), relative_features(cotangent), loss_mask, loss_scale
    )
    gain_full = jnp.zeros_like(gain_grad)
    for dz in range(4):
        gain_full = lax.dynamic_update_slice_in_dim(gain_full, gain_grad[:, dz * row : (dz + 1) * row], (z - dz) % 4 * row, 1)
    grad_gain = gain_full
    for axis, bits in (("dp", (1, 2, 4, 8)), ("tensor", (1, 2, 4))):
        for bit in bits:
            grad_gain = grad_gain + lax.ppermute(grad_gain, axis, [(d, d ^ bit) for d in range(lax.axis_size(axis))])

    joined_grad = joined_grad.astype(BF16)
    blocks = [dz * row + (q ^ dq) * outs for dz in range(4) for dq in range(4)]
    joined_grad = jnp.concatenate([lax.dynamic_slice_in_dim(joined_grad, b, outs, 1) for b in blocks], 1)
    grads = [joined_grad[:, :row]] + [send_z(joined_grad[:, dz * row : (dz + 1) * row], -dz) for dz in (1, 2, 3)]

    near = jnp.concatenate(grads[:2], 0)
    far = jnp.concatenate(grads[2:], 0)
    near_x = jnp.stack([near] + [send_x(near, -dx) for dx in (1, 2, 3)])
    near_all = jnp.stack([near_x, send_y(near_x)]).reshape(-1, row)
    far_y = jnp.stack([far, send_y(far)])
    far_all = jnp.stack([far_y] + [send_x(far_y, -dx) for dx in (1, 2, 3)]).reshape(-1, row)

    features = [jnp.concatenate([low_mids[dz], highs[dz]], 1).reshape(4, 2, part, -1) for dz in range(4)]
    near_features = jnp.stack(features[:2]).transpose(2, 1, 0, 3, 4).reshape(2 * tokens, -1)
    far_features = jnp.stack(features[2:]).transpose(1, 2, 0, 3, 4).reshape(2 * tokens, -1)

    def grad_block(dq):
        columns = slice(dq * outs, (dq + 1) * outs)
        return matmul(near_all[:, columns], near_features, (0, 0)) + matmul(far_all[:, columns], far_features, (0, 0))

    block3 = send_core(grad_block(3).astype(BF16))
    for_pair = send_pair((grad_block(2).astype(BF16).astype(F32) + block3.astype(F32)).astype(BF16))
    block1 = send_core(grad_block(1).astype(BF16))
    own = grad_block(0).astype(BF16).astype(F32) + block1.astype(F32)
    grad_join = (own + for_pair.astype(F32)).reshape(outs, 3, width)
    return (grad_join, grad_gain)


def solution(mesh):
    return jax.shard_map(
        on_device,
        mesh=mesh,
        in_specs=(
            P("dp", "tensor"),
            P("tensor", None),
            P("tensor", None),
            P("dp", "tensor"),
            P("dp", "tensor"),
            P("dp", "tensor"),
            P("dp", None, "tensor"),
            P(),
            P(None, ("dp", "tensor"), None),
            P(("dp", "tensor")),
        ),
        out_specs=(P("dp", None, "tensor"), P()),
        check_vma=False,
    )
```

```python
import jax
import jax.numpy as jnp
from jax import lax
from jax.experimental import pallas as pl
from jax.experimental.pallas import tpu as pltpu
from jax.sharding import PartitionSpec as P

BLOCK = 128
STEPS = 3
EPS = 1e-05
BF16 = jnp.bfloat16
F32 = jnp.float32


def send_x(value, hops):
    pairs = [(x * 2 + y, ((x + hops) % 4) * 2 + y) for x in range(4) for y in range(2)]
    return lax.ppermute(value, "tensor", pairs)


def send_y(value):
    return lax.ppermute(value, "tensor", [(t, t ^ 1) for t in range(8)])


def send_z(value, hops):
    return lax.ppermute(value, "dp", [(d, (d + 4 * hops) % 16) for d in range(16)])


def send_pair(value):
    return lax.ppermute(value, "dp", [(d, d ^ 2) for d in range(16)])


def send_core(value):
    return lax.ppermute(value, "dp", [(d, d ^ 1) for d in range(16)])


def draft_loss(joined_sum, gain_table, cotangent, token_mask, loss_scale):
    current = joined_sum
    running = jnp.zeros((), F32)
    keeper = token_mask.astype(F32)[:, None]
    for step_index in range(STEPS):
        square_mean = jnp.mean(current * current, axis=-1, keepdims=True)
        normed = current * lax.rsqrt(square_mean + EPS) * gain_table[step_index][None, :]
        current = current + jax.nn.silu(normed)
        running = running + jnp.sum(keeper * cotangent[step_index].astype(F32) * current)
    return running * loss_scale


def project_kernel(places_ref, attention_ref, codes_ref, scales_ref, *refs):
    *first_refs, second_other_ref, second_own_ref, weight_ref = refs
    step = pl.program_id(0)
    place = places_ref[step]
    half, blocks = attention_ref.shape[0] // 2, codes_ref.shape[1] // BLOCK
    for k in range(codes_ref.shape[0] // BLOCK):
        for j in range(blocks):
            at = (slice(k * BLOCK, (k + 1) * BLOCK), slice(j * BLOCK, (j + 1) * BLOCK))
            weight_ref[at] = (codes_ref[at].astype(F32) * scales_ref[k, place * blocks + j]).astype(BF16)
    partial = jnp.dot(attention_ref[...], weight_ref[...], preferred_element_type=F32).astype(BF16)
    for index, first_ref in enumerate(first_refs):

        @pl.when(step // 2 == index)
        def _(first_ref=first_ref):
            first_ref[...] = partial[:half]

    @pl.when(step % 2 == 0)
    def _():
        second_other_ref[...] = partial[half:]

    @pl.when(step % 2 == 1)
    def _():
        second_own_ref[...] = partial[half:]


def project(attention, code_blocks, block_scales, places, width):
    rows, depth = attention.shape
    half, steps = rows // 2, places.shape[0]

    def first_spec(index):
        return pl.BlockSpec((None, half, width), lambda step, places: (jnp.clip(step - 2 * index, 0, 1), 0, 0))

    second_spec = pl.BlockSpec((None, half, width), lambda step, places: (places[step] // 2, 0, 0))
    return pl.pallas_call(
        project_kernel,
        grid_spec=pltpu.PrefetchScalarGridSpec(
            num_scalar_prefetch=1,
            grid=(steps,),
            in_specs=[
                pl.BlockSpec((rows, depth), lambda step, places: (0, 0)),
                pl.BlockSpec((depth, width), lambda step, places: (0, places[step])),
                pl.BlockSpec(memory_space=pltpu.SMEM),
            ],
            out_specs=[first_spec(index) for index in range(steps // 2)] + [second_spec] * 2,
            scratch_shapes=[pltpu.VMEM((depth, width), BF16)],
        ),
        out_shape=[jax.ShapeDtypeStruct((2, half, width), BF16)] * (steps // 2)
        + [jax.ShapeDtypeStruct((steps // 2, half, width), BF16)] * 2,
        compiler_params=pltpu.CompilerParams(vmem_limit_bytes=48 * 2**20),
        cost_estimate=pl.CostEstimate(
            flops=2 * rows * depth * width * steps, bytes_accessed=4 * depth * width * steps, transcendentals=0
        ),
    )(places, attention, code_blocks, block_scales)


def matmul(left, right, contract):
    return lax.dot_general(left, right, ((contract[:1], contract[1:]), ((), ())), preferred_element_type=F32)


def on_device(
    attention,
    code_blocks,
    block_scales,
    residual,
    low_feature,
    mid_feature,
    join_weight,
    draft_gain,
    cotangent,
    loss_mask,
):
    dp_index, tensor_index = lax.axis_index("dp"), lax.axis_index("tensor")
    z, q = dp_index // 4, dp_index % 4
    x, y = tensor_index // 2, tensor_index % 2
    tokens, width = residual.shape
    part = tokens // 8
    outs = join_weight.shape[0]

    def pick(value, index, axis):
        return lax.dynamic_index_in_dim(value, index, axis, False)

    z_groups = [[4 * i + j for i in range(4)] for j in range(4)]
    low_all = lax.all_gather(low_feature, "dp", axis_index_groups=z_groups)
    mid_all = lax.all_gather(mid_feature, "dp", axis_index_groups=z_groups)
    weight = jnp.transpose(join_weight, (1, 0, 2))
    weight_pair = send_pair(weight)
    weights = jnp.stack([weight, send_core(weight), weight_pair, send_core(weight_pair)])
    weight_all = jnp.concatenate([pick(weights, q ^ i, 0) for i in range(4)], 1)

    half = tokens // 2
    places = jnp.stack([((x + dx) % 4) * 2 + (y ^ dy) for dx in (2, 1, 3, 0) for dy in (1, 0)])
    *to_send, first_own, to_cross, second_own = project(attention, code_blocks, block_scales, places, width)
    crossed = send_y(to_cross)
    arrived = [send_x(value, dx) for dx, value in zip((2, 1, 3), to_send)]
    first = first_own.astype(F32) + sum(a.astype(F32) for a in arrived)
    second = second_own.astype(F32) + crossed.astype(F32)
    first_other = send_y(first[0].astype(BF16))
    second_other = [send_x(pick(second, (x + dx) % 4, 0).astype(BF16), dx) for dx in (2, 1, 3)]
    residual = residual.astype(F32)
    high_first = residual[:half] + (first[1] + first_other.astype(F32))
    high_second = residual[half:] + (pick(second, x, 0) + sum(a.astype(F32) for a in second_other))
    high = jnp.concatenate([high_first.astype(BF16), high_second.astype(BF16)], 0)

    lows = [pick(low_all, (z + dz) % 4, 0) for dz in range(4)]
    mids = [pick(mid_all, (z + dz) % 4, 0) for dz in range(4)]
    early = [matmul(lows[dz], weight_all[0], (1, 1)) + matmul(mids[dz], weight_all[1], (1, 1)) for dz in range(4)]

    highs = [high] + [send_z(high, -dz) for dz in (1, 2, 3)]
    joined = [(early[dz] + matmul(highs[dz], weight_all[2], (1, 1))).astype(BF16) for dz in range(4)]
    joined = [value.reshape(4, 2, part, -1) for value in joined]

    near = jnp.stack(joined[:2])
    far = jnp.stack(joined[2:])
    near_crossed = send_y(pick(near, 1 - y, 2))
    far_arrived = [send_x(pick(far, (x + dx) % 4, 1), dx) for dx in (2, 1, 3)]
    near_sum = pick(near, y, 2).astype(F32) + near_crossed.astype(F32)
    far_sum = pick(far, x, 1).astype(F32) + sum(a.astype(F32) for a in far_arrived)
    near_other = [send_x(pick(near_sum, (x + dx) % 4, 1).astype(BF16), dx) for dx in (2, 1, 3)]
    far_other = send_y(pick(far_sum, 1 - y, 1).astype(BF16))
    near_total = pick(near_sum, x, 1) + sum(a.astype(F32) for a in near_other)
    far_total = pick(far_sum, y, 1) + far_other.astype(F32)
    totals = [near_total[0]] + [
        send_z(value.astype(BF16), dz).astype(F32)
        for dz, value in ((1, near_total[1]), (2, far_total[0]), (3, far_total[1]))
    ]
    joined_sum = jnp.concatenate(totals, 1)

    row = 4 * outs

    def relative_features(value):
        blocks = [lax.dynamic_slice_in_dim(value, (z - dz) % 4 * row, row, value.ndim - 1) for dz in range(4)]
        return jnp.concatenate(blocks, -1)

    loss_scale = float(tokens * lax.axis_size("dp")) ** (-0.5)
    joined_grad, gain_grad = jax.grad(draft_loss, argnums=(0, 1))(
        joined_sum, relative_features(draft_gain), relative_features(cotangent), loss_mask, loss_scale
    )
    gain_full = jnp.zeros_like(gain_grad)
    for dz in range(4):
        gain_full = lax.dynamic_update_slice_in_dim(gain_full, gain_grad[:, dz * row : (dz + 1) * row], (z - dz) % 4 * row, 1)
    grad_gain = gain_full
    for axis, bits in (("dp", (1, 2, 4, 8)), ("tensor", (1, 2, 4))):
        for bit in bits:
            grad_gain = grad_gain + lax.ppermute(grad_gain, axis, [(d, d ^ bit) for d in range(lax.axis_size(axis))])

    joined_grad = joined_grad.astype(BF16)
    blocks = [dz * row + (q ^ dq) * outs for dz in range(4) for dq in range(4)]
    joined_grad = jnp.concatenate([lax.dynamic_slice_in_dim(joined_grad, b, outs, 1) for b in blocks], 1)
    grads = [joined_grad[:, :row]] + [send_z(joined_grad[:, dz * row : (dz + 1) * row], -dz) for dz in (1, 2, 3)]

    def by_x(pieces):
        gathered = jnp.zeros((4, *pieces[0].shape), BF16)
        for dx, piece in enumerate(pieces):
            gathered = lax.dynamic_update_index_in_dim(gathered, piece, (x + dx) % 4, 0)
        return gathered

    near = jnp.concatenate(grads[:2], 0)
    far = jnp.concatenate(grads[2:], 0)
    near_own = by_x([near] + [send_x(near, -dx) for dx in (1, 2, 3)])
    near_other = send_y(near_own)
    far_pair = jnp.stack([far, send_y(far)])
    far_all = by_x([far_pair] + [send_x(far_pair, -dx) for dx in (1, 2, 3)])

    def by_y(blocks):
        rows = [jnp.concatenate([lows[dz], mids[dz], highs[dz]], 1).reshape(4, 2, part, -1) for dz in blocks]
        return [jnp.stack([pick(r, side, 1) for r in rows], 1) for side in (y, 1 - y)]

    near_features = by_y((0, 1))
    far_features = jnp.stack(by_y((2, 3)), 1)
    terms = [(near_own, near_features[0]), (near_other, near_features[1]), (far_all, far_features)]
    terms = [(left.reshape(-1, row), right.reshape(-1, 3 * width)) for left, right in terms]

    def grad_block(dq):
        columns = slice(dq * outs, (dq + 1) * outs)
        return sum(matmul(left[:, columns], right, (0, 0)) for left, right in terms)

    block3 = send_core(grad_block(3).astype(BF16))
    for_pair = send_pair((grad_block(2).astype(BF16).astype(F32) + block3.astype(F32)).astype(BF16))
    block1 = send_core(grad_block(1).astype(BF16))
    own = grad_block(0).astype(BF16).astype(F32) + block1.astype(F32)
    grad_join = (own + for_pair.astype(F32)).reshape(outs, 3, width)
    return (grad_join, grad_gain)


def solution(mesh):
    return jax.shard_map(
        on_device,
        mesh=mesh,
        in_specs=(
            P("dp", "tensor"),
            P("tensor", None),
            P("tensor", None),
            P("dp", "tensor"),
            P("dp", "tensor"),
            P("dp", "tensor"),
            P("dp", None, "tensor"),
            P(),
            P(None, ("dp", "tensor"), None),
            P(("dp", "tensor")),
        ),
        out_specs=(P("dp", None, "tensor"), P()),
        check_vma=False,
    )
```

```python
import jax
import jax.numpy as jnp
from jax import lax
from jax.experimental import pallas as pl
from jax.experimental.pallas import tpu as pltpu
from jax.sharding import PartitionSpec as P

BLOCK = 128
STEPS = 3
EPS = 1e-05
BF16 = jnp.bfloat16
F32 = jnp.float32


def send_x(value, hops):
    pairs = [(x * 2 + y, ((x + hops) % 4) * 2 + y) for x in range(4) for y in range(2)]
    return lax.ppermute(value, "tensor", pairs)


def send_y(value):
    return lax.ppermute(value, "tensor", [(t, t ^ 1) for t in range(8)])


def send_z(value, hops):
    return lax.ppermute(value, "dp", [(d, (d + 4 * hops) % 16) for d in range(16)])


def send_pair(value):
    return lax.ppermute(value, "dp", [(d, d ^ 2) for d in range(16)])


def send_core(value):
    return lax.ppermute(value, "dp", [(d, d ^ 1) for d in range(16)])


def draft_loss(joined_sum, gain_table, cotangent, token_mask, loss_scale):
    current = joined_sum
    running = jnp.zeros((), F32)
    keeper = token_mask.astype(F32)[:, None]
    for step_index in range(STEPS):
        square_mean = jnp.mean(current * current, axis=-1, keepdims=True)
        normed = current * lax.rsqrt(square_mean + EPS) * gain_table[step_index][None, :]
        current = current + jax.nn.silu(normed)
        running = running + jnp.sum(keeper * cotangent[step_index].astype(F32) * current)
    return running * loss_scale


def project_kernel(places_ref, attention_ref, codes_ref, scales_ref, *refs):
    *first_refs, second_other_ref, second_own_ref, weight_ref = refs
    step = pl.program_id(0)
    place = places_ref[step]
    half, blocks = attention_ref.shape[0] // 2, codes_ref.shape[1] // BLOCK
    for k in range(codes_ref.shape[0] // BLOCK):
        for j in range(blocks):
            at = (slice(k * BLOCK, (k + 1) * BLOCK), slice(j * BLOCK, (j + 1) * BLOCK))
            weight_ref[at] = (codes_ref[at].astype(F32) * scales_ref[k, place * blocks + j]).astype(BF16)
    partial = jnp.dot(attention_ref[...], weight_ref[...], preferred_element_type=F32).astype(BF16)
    for index, first_ref in enumerate(first_refs):

        @pl.when(step // 2 == index)
        def _(first_ref=first_ref):
            first_ref[...] = partial[:half]

    @pl.when(step % 2 == 0)
    def _():
        second_other_ref[...] = partial[half:]

    @pl.when(step % 2 == 1)
    def _():
        second_own_ref[...] = partial[half:]


def project(attention, code_blocks, block_scales, places, width):
    rows, depth = attention.shape
    half, steps = rows // 2, places.shape[0]

    def first_spec(index):
        return pl.BlockSpec((None, half, width), lambda step, places: (jnp.clip(step - 2 * index, 0, 1), 0, 0))

    second_spec = pl.BlockSpec((None, half, width), lambda step, places: (places[step] // 2, 0, 0))
    return pl.pallas_call(
        project_kernel,
        grid_spec=pltpu.PrefetchScalarGridSpec(
            num_scalar_prefetch=1,
            grid=(steps,),
            in_specs=[
                pl.BlockSpec((rows, depth), lambda step, places: (0, 0)),
                pl.BlockSpec((depth, width), lambda step, places: (0, places[step])),
                pl.BlockSpec(memory_space=pltpu.SMEM),
            ],
            out_specs=[first_spec(index) for index in range(steps // 2)] + [second_spec] * 2,
            scratch_shapes=[pltpu.VMEM((depth, width), BF16)],
        ),
        out_shape=[jax.ShapeDtypeStruct((2, half, width), BF16)] * (steps // 2)
        + [jax.ShapeDtypeStruct((steps // 2, half, width), BF16)] * 2,
        compiler_params=pltpu.CompilerParams(vmem_limit_bytes=48 * 2**20),
        cost_estimate=pl.CostEstimate(
            flops=2 * rows * depth * width * steps, bytes_accessed=4 * depth * width * steps, transcendentals=0
        ),
    )(places, attention, code_blocks, block_scales)


def after(value, *others):
    for other in others:
        entry = other[(slice(0, 1),) * other.ndim].reshape(())
        value = value + jnp.minimum(jnp.abs(entry.astype(F32)), 0).astype(value.dtype)
    return value


def matmul(left, right, contract):
    return lax.dot_general(left, right, ((contract[:1], contract[1:]), ((), ())), preferred_element_type=F32)


def on_device(
    attention,
    code_blocks,
    block_scales,
    residual,
    low_feature,
    mid_feature,
    join_weight,
    draft_gain,
    cotangent,
    loss_mask,
):
    dp_index, tensor_index = lax.axis_index("dp"), lax.axis_index("tensor")
    z, q = dp_index // 4, dp_index % 4
    x, y = tensor_index // 2, tensor_index % 2
    tokens, width = residual.shape
    part = tokens // 8
    outs = join_weight.shape[0]

    def pick(value, index, axis):
        return lax.dynamic_index_in_dim(value, index, axis, False)

    low_mid = jnp.concatenate([low_feature, mid_feature], 1)
    low_mids = {0: low_mid, **{dz: send_z(low_mid, -dz) for dz in (1, 3)}}
    weight = jnp.transpose(join_weight, (1, 0, 2))
    weight_pair = jnp.stack([weight, send_pair(weight)])
    weights = jnp.stack([weight_pair, send_core(weight_pair)], 1).reshape(4, *weight.shape)
    weight_all = jnp.concatenate([pick(weights, q ^ i, 0) for i in range(4)], 1)

    half = tokens // 2
    places = jnp.stack([((x + dx) % 4) * 2 + (y ^ dy) for dx in (2, 1, 3, 0) for dy in (1, 0)])
    *to_send, first_own, to_cross, second_own = project(attention, code_blocks, block_scales, places, width)
    crossed = send_y(to_cross)
    to_send = [to_send[0], after(to_send[1], low_mids[1]), after(to_send[2], low_mids[3])]
    low_mids[2] = send_z(after(low_mid, *to_send[1:]), -2)
    arrived = [send_x(value, dx) for dx, value in zip((2, 1, 3), to_send)]
    first = first_own.astype(F32) + sum(a.astype(F32) for a in arrived)
    second = after(second_own.astype(F32) + crossed.astype(F32), low_mids[2])
    first_other = send_y(first[0].astype(BF16))
    second_other = [send_x(pick(second, (x + dx) % 4, 0).astype(BF16), dx) for dx in (2, 1, 3)]
    residual = residual.astype(F32)
    high_first = residual[:half] + (first[1] + first_other.astype(F32))
    high_second = residual[half:] + (pick(second, x, 0) + sum(a.astype(F32) for a in second_other))
    high = jnp.concatenate([high_first.astype(BF16), high_second.astype(BF16)], 0)

    low_mids = [low_mids[dz] for dz in range(4)]
    early = matmul(jnp.concatenate(low_mids, 0), jnp.concatenate([weight_all[0], weight_all[1]], 1), (1, 1))
    early = early.reshape(4, tokens, -1)

    highs = [high] + [send_z(high, -dz) for dz in (1, 2, 3)]
    joined = [(early[dz] + matmul(highs[dz], weight_all[2], (1, 1))).astype(BF16) for dz in range(4)]
    joined = [value.reshape(4, 2, part, -1) for value in joined]

    near = jnp.stack(joined[:2])
    far = jnp.stack(joined[2:])
    near_crossed = send_y(pick(near, 1 - y, 2))
    far_arrived = [send_x(pick(far, (x + dx) % 4, 1), dx) for dx in (2, 1, 3)]
    near_sum = pick(near, y, 2).astype(F32) + near_crossed.astype(F32)
    far_sum = after(pick(far, x, 1).astype(F32) + sum(a.astype(F32) for a in far_arrived), near_sum)
    near_other = [send_x(pick(near_sum, (x + dx) % 4, 1).astype(BF16), dx) for dx in (2, 1, 3)]
    far_other = send_y(pick(far_sum, 1 - y, 1).astype(BF16))
    near_total = pick(near_sum, x, 1) + sum(a.astype(F32) for a in near_other)
    far_total = pick(far_sum, y, 1) + far_other.astype(F32)
    totals = [near_total[0]] + [
        send_z(value.astype(BF16), dz).astype(F32)
        for dz, value in ((1, near_total[1]), (2, far_total[0]), (3, far_total[1]))
    ]
    joined_sum = jnp.concatenate(totals, 1)

    row = 4 * outs

    def relative_features(value):
        blocks = [lax.dynamic_slice_in_dim(value, (z - dz) % 4 * row, row, value.ndim - 1) for dz in range(4)]
        return jnp.concatenate(blocks, -1)

    loss_scale = float(tokens * lax.axis_size("dp")) ** (-0.5)
    joined_grad, gain_grad = jax.grad(draft_loss, argnums=(0, 1))(
        joined_sum, relative_features(draft_gain), relative_features(cotangent), loss_mask, loss_scale
    )
    gain_full = jnp.zeros_like(gain_grad)
    for dz in range(4):
        gain_full = lax.dynamic_update_slice_in_dim(gain_full, gain_grad[:, dz * row : (dz + 1) * row], (z - dz) % 4 * row, 1)
    joined_grad = joined_grad.astype(BF16)
    blocks = [dz * row + (q ^ dq) * outs for dz in range(4) for dq in range(4)]
    joined_grad = jnp.concatenate([lax.dynamic_slice_in_dim(joined_grad, b, outs, 1) for b in blocks], 1)
    grads = [joined_grad[:, :row]] + [send_z(joined_grad[:, dz * row : (dz + 1) * row], -dz) for dz in (1, 2, 3)]

    def by_x(pieces):
        gathered = jnp.zeros((4, *pieces[0].shape), BF16)
        for dx, piece in enumerate(pieces):
            gathered = lax.dynamic_update_index_in_dim(gathered, piece, (x + dx) % 4, 0)
        return gathered

    near = jnp.concatenate(grads[:2], 0)
    far = jnp.concatenate(grads[2:], 0)
    near_x = [near] + [send_x(near, -dx) for dx in (1, 2, 3)]
    near_own = by_x(near_x)
    near_other = send_y(near_own)
    far_pair = jnp.stack([far, send_y(far)])
    far_all = by_x([far_pair] + [send_x(far_pair, -dx) for dx in (1, 2, 3)])

    grad_gain = after(gain_full, near_x[1])
    for axis, bits in (("dp", (1, 2, 4, 8)), ("tensor", (1, 2, 4))):
        for bit in bits:
            grad_gain = grad_gain + lax.ppermute(grad_gain, axis, [(d, d ^ bit) for d in range(lax.axis_size(axis))])

    def by_y(blocks):
        rows = [jnp.concatenate([low_mids[dz], highs[dz]], 1).reshape(4, 2, part, -1) for dz in blocks]
        return [jnp.stack([pick(r, side, 1) for r in rows], 1) for side in (y, 1 - y)]

    near_features = by_y((0, 1))
    far_features = jnp.stack(by_y((2, 3)), 1)
    terms = [(near_own, near_features[0]), (near_other, near_features[1]), (far_all, far_features)]
    terms = [(left.reshape(-1, row), right.reshape(-1, 3 * width)) for left, right in terms]

    def grad_block(dq):
        columns = slice(dq * outs, (dq + 1) * outs)
        return sum(matmul(left[:, columns], right, (0, 0)) for left, right in terms)

    block3 = send_core(grad_block(3).astype(BF16))
    for_pair = send_pair((grad_block(2).astype(BF16).astype(F32) + block3.astype(F32)).astype(BF16))
    block1 = send_core(grad_block(1).astype(BF16))
    own = grad_block(0).astype(BF16).astype(F32) + block1.astype(F32)
    grad_join = (own + for_pair.astype(F32)).reshape(outs, 3, width)
    return (grad_join, grad_gain)


def solution(mesh):
    return jax.shard_map(
        on_device,
        mesh=mesh,
        in_specs=(
            P("dp", "tensor"),
            P("tensor", None),
            P("tensor", None),
            P("dp", "tensor"),
            P("dp", "tensor"),
            P("dp", "tensor"),
            P("dp", None, "tensor"),
            P(),
            P(None, ("dp", "tensor"), None),
            P(("dp", "tensor")),
        ),
        out_specs=(P("dp", None, "tensor"), P()),
        check_vma=False,
    )
```

```python
import jax
import jax.numpy as jnp
from jax import lax
from jax.experimental import pallas as pl
from jax.experimental.pallas import tpu as pltpu
from jax.sharding import PartitionSpec as P

BLOCK = 128
STEPS = 3
EPS = 1e-05
BF16 = jnp.bfloat16
F32 = jnp.float32


def send_x(value, hops):
    pairs = [(x * 2 + y, ((x + hops) % 4) * 2 + y) for x in range(4) for y in range(2)]
    return lax.ppermute(value, "tensor", pairs)


def send_y(value):
    return lax.ppermute(value, "tensor", [(t, t ^ 1) for t in range(8)])


def send_z(value, hops):
    return lax.ppermute(value, "dp", [(d, (d + 4 * hops) % 16) for d in range(16)])


def send_pair(value):
    return lax.ppermute(value, "dp", [(d, d ^ 2) for d in range(16)])


def send_core(value):
    return lax.ppermute(value, "dp", [(d, d ^ 1) for d in range(16)])


def draft_loss(joined_sum, gain_table, cotangent, token_mask, loss_scale):
    current = joined_sum
    running = jnp.zeros((), F32)
    keeper = token_mask.astype(F32)[:, None]
    for step_index in range(STEPS):
        square_mean = jnp.mean(current * current, axis=-1, keepdims=True)
        normed = current * lax.rsqrt(square_mean + EPS) * gain_table[step_index][None, :]
        current = current + jax.nn.silu(normed)
        running = running + jnp.sum(keeper * cotangent[step_index].astype(F32) * current)
    return running * loss_scale


def project_kernel(places_ref, attention_ref, codes_ref, scales_ref, *refs):
    *first_refs, second_other_ref, second_own_ref, weight_ref = refs
    step = pl.program_id(0)
    place = places_ref[step]
    half, blocks = attention_ref.shape[0] // 2, codes_ref.shape[1] // BLOCK
    for k in range(codes_ref.shape[0] // BLOCK):
        for j in range(blocks):
            at = (slice(k * BLOCK, (k + 1) * BLOCK), slice(j * BLOCK, (j + 1) * BLOCK))
            weight_ref[at] = (codes_ref[at].astype(F32) * scales_ref[k, place * blocks + j]).astype(BF16)
    partial = jnp.dot(attention_ref[...], weight_ref[...], preferred_element_type=F32).astype(BF16)
    for index, first_ref in enumerate(first_refs):

        @pl.when(step // 2 == index)
        def _(first_ref=first_ref):
            first_ref[...] = partial[:half]

    @pl.when(step % 2 == 0)
    def _():
        second_other_ref[...] = partial[half:]

    @pl.when(step % 2 == 1)
    def _():
        second_own_ref[...] = partial[half:]


def project(attention, code_blocks, block_scales, places, width):
    rows, depth = attention.shape
    half, steps = rows // 2, places.shape[0]

    def first_spec(index):
        return pl.BlockSpec((None, half, width), lambda step, places: (jnp.clip(step - 2 * index, 0, 1), 0, 0))

    second_spec = pl.BlockSpec((None, half, width), lambda step, places: (places[step] // 2, 0, 0))
    return pl.pallas_call(
        project_kernel,
        grid_spec=pltpu.PrefetchScalarGridSpec(
            num_scalar_prefetch=1,
            grid=(steps,),
            in_specs=[
                pl.BlockSpec((rows, depth), lambda step, places: (0, 0)),
                pl.BlockSpec((depth, width), lambda step, places: (0, places[step])),
                pl.BlockSpec(memory_space=pltpu.SMEM),
            ],
            out_specs=[first_spec(index) for index in range(steps // 2)] + [second_spec] * 2,
            scratch_shapes=[pltpu.VMEM((depth, width), BF16)],
        ),
        out_shape=[jax.ShapeDtypeStruct((2, half, width), BF16)] * (steps // 2)
        + [jax.ShapeDtypeStruct((steps // 2, half, width), BF16)] * 2,
        compiler_params=pltpu.CompilerParams(vmem_limit_bytes=48 * 2**20),
        cost_estimate=pl.CostEstimate(
            flops=2 * rows * depth * width * steps, bytes_accessed=4 * depth * width * steps, transcendentals=0
        ),
    )(places, attention, code_blocks, block_scales)


def after(value, *others):
    for other in others:
        entry = other[(slice(0, 1),) * other.ndim].reshape(())
        value = value + jnp.minimum(jnp.abs(entry.astype(F32)), 0).astype(value.dtype)
    return value


def matmul(left, right, contract):
    return lax.dot_general(left, right, ((contract[:1], contract[1:]), ((), ())), preferred_element_type=F32)


def on_device(
    attention,
    code_blocks,
    block_scales,
    residual,
    low_feature,
    mid_feature,
    join_weight,
    draft_gain,
    cotangent,
    loss_mask,
):
    dp_index, tensor_index = lax.axis_index("dp"), lax.axis_index("tensor")
    z, q = dp_index // 4, dp_index % 4
    x, y = tensor_index // 2, tensor_index % 2
    tokens, width = residual.shape
    part = tokens // 8
    outs = join_weight.shape[0]

    def pick(value, index, axis):
        return lax.dynamic_index_in_dim(value, index, axis, False)

    low_mid = jnp.stack([low_feature, mid_feature])
    low_mids = {0: low_mid, **{dz: send_z(low_mid, -dz) for dz in (1, 3)}}
    weight = jnp.transpose(join_weight, (1, 0, 2))
    weight_pair = jnp.stack([weight, send_pair(weight)])
    weights = jnp.stack([weight_pair, send_core(weight_pair)], 1).reshape(4, *weight.shape)
    weight_all = jnp.concatenate([pick(weights, q ^ i, 0) for i in range(4)], 1)

    half = tokens // 2
    places = jnp.stack([((x + dx) % 4) * 2 + (y ^ dy) for dx in (2, 1, 3, 0) for dy in (1, 0)])
    *to_send, first_own, to_cross, second_own = project(attention, code_blocks, block_scales, places, width)
    crossed = send_y(to_cross)
    to_send = [to_send[0], after(to_send[1], low_mids[1]), after(to_send[2], low_mids[3])]
    low_mids[2] = send_z(after(low_mid, *to_send[1:]), -2)
    arrived = [send_x(value, dx) for dx, value in zip((2, 1, 3), to_send)]
    first = first_own.astype(F32) + sum(a.astype(F32) for a in arrived)
    second = second_own.astype(F32) + crossed.astype(F32)
    first_other = send_y(first[0].astype(BF16))
    second_other = [send_x(pick(second, (x + dx) % 4, 0).astype(BF16), dx) for dx in (2, 1, 3)]
    residual = residual.astype(F32)
    high_first = residual[:half] + (first[1] + first_other.astype(F32))
    high_second = residual[half:] + (pick(second, x, 0) + sum(a.astype(F32) for a in second_other))
    high_second = after(high_second, low_mids[2])
    high = jnp.concatenate([high_first.astype(BF16), high_second.astype(BF16)], 0)

    low_mids = [low_mids[dz] for dz in range(4)]
    early = [jnp.concatenate([value[kind] for value in low_mids], 0) for kind in range(2)]
    early = matmul(early[0], weight_all[0], (1, 1)) + matmul(early[1], weight_all[1], (1, 1))
    early = early.reshape(4, tokens, -1)

    highs = {0: high, 1: send_z(high, -1), 3: send_z(high, -3)}
    highs[2] = send_z(after(high, highs[1]), -2)
    joined = [(early[dz] + matmul(highs[dz], weight_all[2], (1, 1))).astype(BF16) for dz in range(4)]
    joined = [value.reshape(4, 2, part, -1) for value in joined]

    near = jnp.stack(joined[:2])
    far = jnp.stack(joined[2:])
    near_crossed = send_y(pick(near, 1 - y, 2))
    far_arrived = [send_x(pick(far, (x + dx) % 4, 1), dx) for dx in (2, 1, 3)]
    near_sum = pick(near, y, 2).astype(F32) + near_crossed.astype(F32)
    far_sum = after(pick(far, x, 1).astype(F32) + sum(a.astype(F32) for a in far_arrived), near_sum)
    near_other = [send_x(pick(near_sum, (x + dx) % 4, 1).astype(BF16), dx) for dx in (2, 1, 3)]
    far_other = send_y(pick(far_sum, 1 - y, 1).astype(BF16))
    near_total = pick(near_sum, x, 1) + sum(a.astype(F32) for a in near_other)
    far_total = pick(far_sum, y, 1) + far_other.astype(F32)
    totals = [near_total[0]] + [
        send_z(value.astype(BF16), dz).astype(F32)
        for dz, value in ((1, near_total[1]), (2, far_total[0]), (3, far_total[1]))
    ]
    joined_sum = jnp.concatenate(totals, 1)

    row = 4 * outs

    def relative_features(value):
        blocks = [lax.dynamic_slice_in_dim(value, (z - dz) % 4 * row, row, value.ndim - 1) for dz in range(4)]
        return jnp.concatenate(blocks, -1)

    loss_scale = float(tokens * lax.axis_size("dp")) ** (-0.5)
    joined_grad, gain_grad = jax.grad(draft_loss, argnums=(0, 1))(
        joined_sum, relative_features(draft_gain), relative_features(cotangent), loss_mask, loss_scale
    )
    gain_full = jnp.zeros_like(gain_grad)
    for dz in range(4):
        gain_full = lax.dynamic_update_slice_in_dim(gain_full, gain_grad[:, dz * row : (dz + 1) * row], (z - dz) % 4 * row, 1)
    joined_grad = joined_grad.astype(BF16)
    blocks = [dz * row + (q ^ dq) * outs for dz in range(4) for dq in range(4)]
    joined_grad = jnp.concatenate([lax.dynamic_slice_in_dim(joined_grad, b, outs, 1) for b in blocks], 1)
    grads = [joined_grad[:, :row]] + [send_z(joined_grad[:, dz * row : (dz + 1) * row], -dz) for dz in (1, 2, 3)]

    def by_x(pieces):
        gathered = jnp.zeros((4, *pieces[0].shape), BF16)
        for dx, piece in enumerate(pieces):
            gathered = lax.dynamic_update_index_in_dim(gathered, piece, (x + dx) % 4, 0)
        return gathered

    near = jnp.concatenate(grads[:2], 0)
    far = jnp.concatenate(grads[2:], 0)
    near_x = [near] + [send_x(near, -dx) for dx in (1, 2, 3)]
    near_own = by_x(near_x)
    pieces = jnp.stack([near, far])
    crossed = send_y(pieces)
    far_pair = jnp.stack([far, crossed[1]])
    far_all = by_x([far_pair] + [send_x(far_pair, -dx) for dx in (1, 2, 3)])
    rest = send_y(jnp.stack(near_x[1:]))
    near_other = by_x([crossed[0], rest[0], rest[1], rest[2]])

    grad_gain = after(gain_full, crossed)
    for axis, bits in (("dp", (1, 2, 4, 8)), ("tensor", (1, 2, 4))):
        for bit in bits:
            grad_gain = grad_gain + lax.ppermute(grad_gain, axis, [(d, d ^ bit) for d in range(lax.axis_size(axis))])

    def by_y(blocks):
        rows = [jnp.concatenate([low_mids[dz][0], low_mids[dz][1], highs[dz]], 1).reshape(4, 2, part, -1) for dz in blocks]
        return [jnp.stack([pick(r, side, 1) for r in rows], 1) for side in (y, 1 - y)]

    near_features = by_y((0, 1))
    far_features = jnp.stack(by_y((2, 3)), 1)
    terms = [(near_own, near_features[0]), (near_other, near_features[1]), (far_all, far_features)]
    terms = [(left.reshape(-1, row), right.reshape(-1, 3 * width)) for left, right in terms]

    def grad_block(dq):
        columns = slice(dq * outs, (dq + 1) * outs)
        return sum(matmul(left[:, columns], right, (0, 0)) for left, right in terms)

    block3 = send_core(grad_block(3).astype(BF16))
    for_pair = send_pair((grad_block(2).astype(BF16).astype(F32) + block3.astype(F32)).astype(BF16))
    block1 = send_core(grad_block(1).astype(BF16))
    own = grad_block(0).astype(BF16).astype(F32) + block1.astype(F32)
    kinds = [slice(kind * width, (kind + 1) * width) for kind in range(3)]
    grad_join = jnp.stack([own[:, k] + for_pair[:, k].astype(F32) for k in kinds]).transpose(1, 0, 2)
    return (grad_join, grad_gain)


def solution(mesh):
    return jax.shard_map(
        on_device,
        mesh=mesh,
        in_specs=(
            P("dp", "tensor"),
            P("tensor", None),
            P("tensor", None),
            P("dp", "tensor"),
            P("dp", "tensor"),
            P("dp", "tensor"),
            P("dp", None, "tensor"),
            P(),
            P(None, ("dp", "tensor"), None),
            P(("dp", "tensor")),
        ),
        out_specs=(P("dp", None, "tensor"), P()),
        check_vma=False,
    )
```

```python
import jax
import jax.numpy as jnp
from jax import lax
from jax.experimental import pallas as pl
from jax.experimental.pallas import tpu as pltpu
from jax.sharding import PartitionSpec as P

BLOCK = 128
STEPS = 3
EPS = 1e-05
BF16 = jnp.bfloat16
F32 = jnp.float32


def send_x(value, hops):
    pairs = [(x * 2 + y, ((x + hops) % 4) * 2 + y) for x in range(4) for y in range(2)]
    return lax.ppermute(value, "tensor", pairs)


def send_y(value):
    return lax.ppermute(value, "tensor", [(t, t ^ 1) for t in range(8)])


def send_z(value, hops):
    return lax.ppermute(value, "dp", [(d, (d + 4 * hops) % 16) for d in range(16)])


def send_pair(value):
    return lax.ppermute(value, "dp", [(d, d ^ 2) for d in range(16)])


def send_core(value):
    return lax.ppermute(value, "dp", [(d, d ^ 1) for d in range(16)])


def draft_loss(joined_sum, gain_table, cotangent, token_mask, loss_scale):
    current = joined_sum
    running = jnp.zeros((), F32)
    keeper = token_mask.astype(F32)[:, None]
    for step_index in range(STEPS):
        square_mean = jnp.mean(current * current, axis=-1, keepdims=True)
        normed = current * lax.rsqrt(square_mean + EPS) * gain_table[step_index][None, :]
        current = current + jax.nn.silu(normed)
        running = running + jnp.sum(keeper * cotangent[step_index].astype(F32) * current)
    return running * loss_scale


def project_kernel(places_ref, attention_ref, codes_ref, scales_ref, *refs):
    *first_refs, second_other_ref, second_own_ref, weight_ref = refs
    step = pl.program_id(0)
    place = places_ref[step]
    half, blocks = attention_ref.shape[0] // 2, codes_ref.shape[1] // BLOCK
    for k in range(codes_ref.shape[0] // BLOCK):
        for j in range(blocks):
            at = (slice(k * BLOCK, (k + 1) * BLOCK), slice(j * BLOCK, (j + 1) * BLOCK))
            weight_ref[at] = (codes_ref[at].astype(F32) * scales_ref[k, place * blocks + j]).astype(BF16)
    partial = jnp.dot(attention_ref[...], weight_ref[...], preferred_element_type=F32).astype(BF16)
    for index, first_ref in enumerate(first_refs):

        @pl.when(step // 2 == index)
        def _(first_ref=first_ref):
            first_ref[...] = partial[:half]

    @pl.when(step % 2 == 0)
    def _():
        second_other_ref[...] = partial[half:]

    @pl.when(step % 2 == 1)
    def _():
        second_own_ref[...] = partial[half:]


def project(attention, code_blocks, block_scales, places, width):
    rows, depth = attention.shape
    half, steps = rows // 2, places.shape[0]

    def first_spec(index):
        return pl.BlockSpec((None, half, width), lambda step, places: (jnp.clip(step - 2 * index, 0, 1), 0, 0))

    second_spec = pl.BlockSpec((None, half, width), lambda step, places: (places[step] // 2, 0, 0))
    return pl.pallas_call(
        project_kernel,
        grid_spec=pltpu.PrefetchScalarGridSpec(
            num_scalar_prefetch=1,
            grid=(steps,),
            in_specs=[
                pl.BlockSpec((rows, depth), lambda step, places: (0, 0)),
                pl.BlockSpec((depth, width), lambda step, places: (0, places[step])),
                pl.BlockSpec(memory_space=pltpu.SMEM),
            ],
            out_specs=[first_spec(index) for index in range(steps // 2)] + [second_spec] * 2,
            scratch_shapes=[pltpu.VMEM((depth, width), BF16)],
        ),
        out_shape=[jax.ShapeDtypeStruct((2, half, width), BF16)] * (steps // 2)
        + [jax.ShapeDtypeStruct((steps // 2, half, width), BF16)] * 2,
        compiler_params=pltpu.CompilerParams(vmem_limit_bytes=48 * 2**20),
        cost_estimate=pl.CostEstimate(
            flops=2 * rows * depth * width * steps, bytes_accessed=4 * depth * width * steps, transcendentals=0
        ),
    )(places, attention, code_blocks, block_scales)


def after(value, *others):
    for other in others:
        entry = other[(slice(0, 1),) * other.ndim].reshape(())
        value = value + jnp.minimum(jnp.abs(entry.astype(F32)), 0).astype(value.dtype)
    return value


def matmul(left, right, contract):
    return lax.dot_general(left, right, ((contract[:1], contract[1:]), ((), ())), preferred_element_type=F32)


def on_device(
    attention,
    code_blocks,
    block_scales,
    residual,
    low_feature,
    mid_feature,
    join_weight,
    draft_gain,
    cotangent,
    loss_mask,
):
    dp_index, tensor_index = lax.axis_index("dp"), lax.axis_index("tensor")
    z, q = dp_index // 4, dp_index % 4
    x, y = tensor_index // 2, tensor_index % 2
    tokens, width = residual.shape
    part = tokens // 8
    outs = join_weight.shape[0]

    def pick(value, index, axis):
        return lax.dynamic_index_in_dim(value, index, axis, False)

    low_mid = jnp.stack([low_feature, mid_feature])
    low_mids = {0: low_mid, **{dz: send_z(low_mid, -dz) for dz in (1, 3)}}
    weight = jnp.transpose(join_weight, (1, 0, 2))
    weight_pair = jnp.stack([weight, send_pair(weight)])
    half = tokens // 2
    places = jnp.stack([((x + dx) % 4) * 2 + (y ^ dy) for dx in (2, 1, 3, 0) for dy in (1, 0)])
    *to_send, first_own, to_cross, second_own = project(attention, code_blocks, block_scales, places, width)
    crossed = send_y(to_cross)
    to_send = [to_send[0], after(to_send[1], low_mids[1]), after(to_send[2], low_mids[3])]
    low_mids[2] = send_z(after(low_mid, *to_send[1:], weight_pair[1]), -2)
    weight_core = send_core(after(weight_pair, low_mids[2]))
    weights = jnp.stack([weight_pair, weight_core], 1).reshape(4, *weight.shape)
    weight_all = jnp.concatenate([pick(weights, q ^ i, 0) for i in range(4)], 1)
    arrived = [send_x(value, dx) for dx, value in zip((2, 1, 3), to_send)]
    first = first_own.astype(F32) + sum(a.astype(F32) for a in arrived)
    second = second_own.astype(F32) + crossed.astype(F32)
    first_other = send_y(first[0].astype(BF16))
    second_other = [send_x(pick(second, (x + dx) % 4, 0).astype(BF16), dx) for dx in (2, 1, 3)]
    residual = residual.astype(F32)
    high_first = residual[:half] + (first[1] + first_other.astype(F32))
    high_second = residual[half:] + (pick(second, x, 0) + sum(a.astype(F32) for a in second_other))
    high_second = after(high_second, weight_core)
    high = jnp.concatenate([high_first.astype(BF16), high_second.astype(BF16)], 0)

    low_mids = [low_mids[dz] for dz in range(4)]
    early = [jnp.concatenate([value[kind] for value in low_mids], 0) for kind in range(2)]
    early = matmul(early[0], weight_all[0], (1, 1)) + matmul(early[1], weight_all[1], (1, 1))
    early = early.reshape(4, tokens, -1)

    highs = {0: high, 1: send_z(high, -1), 3: send_z(high, -3)}
    highs[2] = send_z(after(high, highs[1]), -2)
    joined = [(early[dz] + matmul(highs[dz], weight_all[2], (1, 1))).astype(BF16) for dz in range(4)]
    joined = [value.reshape(4, 2, part, -1) for value in joined]

    near = jnp.stack(joined[:2])
    far = jnp.stack(joined[2:])
    near_crossed = send_y(pick(near, 1 - y, 2))
    far_arrived = [send_x(pick(far, (x + dx) % 4, 1), dx) for dx in (2, 1, 3)]
    near_sum = pick(near, y, 2).astype(F32) + near_crossed.astype(F32)
    far_sum = after(pick(far, x, 1).astype(F32) + sum(a.astype(F32) for a in far_arrived), near_sum)
    near_other = [send_x(pick(near_sum, (x + dx) % 4, 1).astype(BF16), dx) for dx in (2, 1, 3)]
    far_other = send_y(pick(far_sum, 1 - y, 1).astype(BF16))
    near_total = pick(near_sum, x, 1) + sum(a.astype(F32) for a in near_other)
    far_total = pick(far_sum, y, 1) + far_other.astype(F32)
    totals = [near_total[0]] + [
        send_z(value.astype(BF16), dz).astype(F32)
        for dz, value in ((1, near_total[1]), (2, far_total[0]), (3, far_total[1]))
    ]
    joined_sum = jnp.concatenate(totals, 1)

    row = 4 * outs

    def relative_features(value):
        blocks = [lax.dynamic_slice_in_dim(value, (z - dz) % 4 * row, row, value.ndim - 1) for dz in range(4)]
        return jnp.concatenate(blocks, -1)

    loss_scale = float(tokens * lax.axis_size("dp")) ** (-0.5)
    joined_grad, gain_grad = jax.grad(draft_loss, argnums=(0, 1))(
        joined_sum, relative_features(draft_gain), relative_features(cotangent), loss_mask, loss_scale
    )
    gain_full = jnp.zeros_like(gain_grad)
    for dz in range(4):
        gain_full = lax.dynamic_update_slice_in_dim(gain_full, gain_grad[:, dz * row : (dz + 1) * row], (z - dz) % 4 * row, 1)
    joined_grad = joined_grad.astype(BF16)
    blocks = [dz * row + (q ^ dq) * outs for dz in range(4) for dq in range(4)]
    joined_grad = jnp.concatenate([lax.dynamic_slice_in_dim(joined_grad, b, outs, 1) for b in blocks], 1)
    grads = [joined_grad[:, :row]] + [send_z(joined_grad[:, dz * row : (dz + 1) * row], -dz) for dz in (1, 2, 3)]

    def by_x(pieces):
        gathered = jnp.zeros((4, *pieces[0].shape), BF16)
        for dx, piece in enumerate(pieces):
            gathered = lax.dynamic_update_index_in_dim(gathered, piece, (x + dx) % 4, 0)
        return gathered

    near = jnp.concatenate(grads[:2], 0)
    far = jnp.concatenate(grads[2:], 0)
    near_x = [near] + [send_x(near, -dx) for dx in (1, 2, 3)]
    near_own = by_x(near_x)
    pieces = jnp.stack([near, far])
    crossed = send_y(pieces)
    far_pair = jnp.stack([far, crossed[1]])
    far_x = [far_pair] + [send_x(far_pair, -dx) for dx in (1, 2, 3)]
    far_all = by_x(far_x)
    rest = send_y(jnp.stack(near_x[1:]))
    near_other = by_x([crossed[0], rest[0], rest[1], rest[2]])

    def by_y(blocks):
        rows = [jnp.concatenate([low_mids[dz][0], low_mids[dz][1], highs[dz]], 1).reshape(4, 2, part, -1) for dz in blocks]
        return [jnp.stack([pick(r, side, 1) for r in rows], 1) for side in (y, 1 - y)]

    near_features = by_y((0, 1))
    far_features = jnp.stack(by_y((2, 3)), 1)
    terms = [(near_own, near_features[0]), (near_other, near_features[1]), (far_all, far_features)]
    terms = [(left.reshape(-1, row), right.reshape(-1, 3 * width)) for left, right in terms]

    def grad_block(dq):
        columns = slice(dq * outs, (dq + 1) * outs)
        return sum(matmul(left[:, columns], right, (0, 0)) for left, right in terms)

    block3 = send_core(grad_block(3).astype(BF16))
    pair_sum = (grad_block(2).astype(BF16).astype(F32) + block3.astype(F32)).astype(BF16)
    for_pair = send_pair(pair_sum)

    grad_gain = gain_full
    stages = [("dp", 1, crossed), ("dp", 2, far_x[1]), ("dp", 4, None), ("dp", 8, pair_sum)]
    stages += [("tensor", 1, None), ("tensor", 2, None), ("tensor", 4, None)]
    for axis, bit, earlier in stages:
        grad_gain = grad_gain if earlier is None else after(grad_gain, earlier)
        grad_gain = grad_gain + lax.ppermute(grad_gain, axis, [(d, d ^ bit) for d in range(lax.axis_size(axis))])

    block1 = send_core(grad_block(1).astype(BF16))
    own = grad_block(0).astype(BF16).astype(F32) + block1.astype(F32)
    kinds = [slice(kind * width, (kind + 1) * width) for kind in range(3)]
    grad_join = jnp.stack([own[:, k] + for_pair[:, k].astype(F32) for k in kinds]).transpose(1, 0, 2)
    return (grad_join, grad_gain)


def solution(mesh):
    return jax.shard_map(
        on_device,
        mesh=mesh,
        in_specs=(
            P("dp", "tensor"),
            P("tensor", None),
            P("tensor", None),
            P("dp", "tensor"),
            P("dp", "tensor"),
            P("dp", "tensor"),
            P("dp", None, "tensor"),
            P(),
            P(None, ("dp", "tensor"), None),
            P(("dp", "tensor")),
        ),
        out_specs=(P("dp", None, "tensor"), P()),
        check_vma=False,
    )
```

```python
import jax
import jax.numpy as jnp
from jax import lax
from jax.experimental import pallas as pl
from jax.experimental.pallas import tpu as pltpu
from jax.sharding import PartitionSpec as P

BLOCK = 128
STEPS = 3
EPS = 1e-05
BF16 = jnp.bfloat16
F32 = jnp.float32


def send_x(value, hops):
    pairs = [(x * 2 + y, ((x + hops) % 4) * 2 + y) for x in range(4) for y in range(2)]
    return lax.ppermute(value, "tensor", pairs)


def send_y(value):
    return lax.ppermute(value, "tensor", [(t, t ^ 1) for t in range(8)])


def send_z(value, hops):
    return lax.ppermute(value, "dp", [(d, (d + 4 * hops) % 16) for d in range(16)])


def send_pair(value):
    return lax.ppermute(value, "dp", [(d, d ^ 2) for d in range(16)])


def send_core(value):
    return lax.ppermute(value, "dp", [(d, d ^ 1) for d in range(16)])


def draft_loss(joined_sum, gain_table, cotangent, token_mask, loss_scale):
    current = joined_sum
    running = jnp.zeros((), F32)
    keeper = token_mask.astype(F32)[:, None]
    for step_index in range(STEPS):
        square_mean = jnp.mean(current * current, axis=-1, keepdims=True)
        normed = current * lax.rsqrt(square_mean + EPS) * gain_table[step_index][None, :]
        current = current + jax.nn.silu(normed)
        running = running + jnp.sum(keeper * cotangent[step_index].astype(F32) * current)
    return running * loss_scale


def project_kernel(places_ref, attention_ref, codes_ref, scales_ref, *refs):
    *first_refs, second_other_ref, second_own_ref, weight_ref = refs
    step = pl.program_id(0)
    place = places_ref[step]
    half, blocks = attention_ref.shape[0] // 2, codes_ref.shape[1] // BLOCK
    for k in range(codes_ref.shape[0] // BLOCK):
        for j in range(blocks):
            at = (slice(k * BLOCK, (k + 1) * BLOCK), slice(j * BLOCK, (j + 1) * BLOCK))
            weight_ref[at] = (codes_ref[at].astype(F32) * scales_ref[k, place * blocks + j]).astype(BF16)
    partial = jnp.dot(attention_ref[...], weight_ref[...], preferred_element_type=F32).astype(BF16)
    for index, first_ref in enumerate(first_refs):

        @pl.when(step // 2 == index)
        def _(first_ref=first_ref):
            first_ref[...] = partial[:half]

    @pl.when(step % 2 == 0)
    def _():
        second_other_ref[...] = partial[half:]

    @pl.when(step % 2 == 1)
    def _():
        second_own_ref[...] = partial[half:]


def project(attention, code_blocks, block_scales, places, width):
    rows, depth = attention.shape
    half, steps = rows // 2, places.shape[0]

    def first_spec(index):
        return pl.BlockSpec((None, half, width), lambda step, places: (jnp.clip(step - 2 * index, 0, 1), 0, 0))

    second_spec = pl.BlockSpec((None, half, width), lambda step, places: (places[step] // 2, 0, 0))
    return pl.pallas_call(
        project_kernel,
        grid_spec=pltpu.PrefetchScalarGridSpec(
            num_scalar_prefetch=1,
            grid=(steps,),
            in_specs=[
                pl.BlockSpec((rows, depth), lambda step, places: (0, 0)),
                pl.BlockSpec((depth, width), lambda step, places: (0, places[step])),
                pl.BlockSpec(memory_space=pltpu.SMEM),
            ],
            out_specs=[first_spec(index) for index in range(steps // 2)] + [second_spec] * 2,
            scratch_shapes=[pltpu.VMEM((depth, width), BF16)],
        ),
        out_shape=[jax.ShapeDtypeStruct((2, half, width), BF16)] * (steps // 2)
        + [jax.ShapeDtypeStruct((steps // 2, half, width), BF16)] * 2,
        compiler_params=pltpu.CompilerParams(vmem_limit_bytes=48 * 2**20),
        cost_estimate=pl.CostEstimate(
            flops=2 * rows * depth * width * steps, bytes_accessed=4 * depth * width * steps, transcendentals=0
        ),
    )(places, attention, code_blocks, block_scales)


def after(value, *others):
    for other in others:
        entry = other[(slice(0, 1),) * other.ndim].reshape(())
        value = value + jnp.minimum(jnp.abs(entry.astype(F32)), 0).astype(value.dtype)
    return value


def matmul(left, right, contract):
    return lax.dot_general(left, right, ((contract[:1], contract[1:]), ((), ())), preferred_element_type=F32)


def on_device(
    attention,
    code_blocks,
    block_scales,
    residual,
    low_feature,
    mid_feature,
    join_weight,
    draft_gain,
    cotangent,
    loss_mask,
):
    dp_index, tensor_index = lax.axis_index("dp"), lax.axis_index("tensor")
    z, q = dp_index // 4, dp_index % 4
    x, y = tensor_index // 2, tensor_index % 2
    tokens, width = residual.shape
    part = tokens // 8
    outs = join_weight.shape[0]

    def pick(value, index, axis):
        return lax.dynamic_index_in_dim(value, index, axis, False)

    low_mid = jnp.stack([low_feature, mid_feature])
    low_mids = {0: low_mid, **{dz: send_z(low_mid, -dz) for dz in (1, 3)}}
    weight = jnp.transpose(join_weight, (1, 0, 2))
    weight_pair = jnp.stack([weight, send_pair(weight)])
    weights = jnp.stack([weight_pair, send_core(weight_pair)], 1).reshape(4, *weight.shape)
    weight_all = jnp.concatenate([pick(weights, q ^ i, 0) for i in range(4)], 1)

    half = tokens // 2
    places = jnp.stack([((x + dx) % 4) * 2 + (y ^ dy) for dx in (2, 1, 3, 0) for dy in (1, 0)])
    *to_send, first_own, to_cross, second_own = project(attention, code_blocks, block_scales, places, width)
    crossed = send_y(to_cross)
    to_send = [to_send[0], after(to_send[1], low_mids[1]), after(to_send[2], low_mids[3])]
    low_mids[2] = send_z(after(low_mid, *to_send[1:]), -2)
    arrived = [send_x(value, dx) for dx, value in zip((2, 1, 3), to_send)]
    first = first_own.astype(F32) + sum(a.astype(F32) for a in arrived)
    second = second_own.astype(F32) + crossed.astype(F32)
    first_other = send_y(first[0].astype(BF16))
    second_other = [send_x(pick(second, (x + dx) % 4, 0).astype(BF16), dx) for dx in (2, 1, 3)]
    residual = residual.astype(F32)
    high_first = residual[:half] + (first[1] + first_other.astype(F32))
    high_second = residual[half:] + (pick(second, x, 0) + sum(a.astype(F32) for a in second_other))
    high_second = after(high_second, low_mids[2])
    high = jnp.concatenate([high_first.astype(BF16), high_second.astype(BF16)], 0)

    low_mids = [low_mids[dz] for dz in range(4)]
    early = [jnp.concatenate([value[kind] for value in low_mids], 0) for kind in range(2)]
    early = matmul(early[0], weight_all[0], (1, 1)) + matmul(early[1], weight_all[1], (1, 1))
    early = early.reshape(4, tokens, -1)

    highs = {0: high, 1: send_z(high, -1), 3: send_z(high, -3)}
    highs[2] = send_z(after(high, highs[1]), -2)
    joined = [(early[dz] + matmul(highs[dz], weight_all[2], (1, 1))).astype(BF16) for dz in range(4)]
    joined = [value.reshape(4, 2, part, -1) for value in joined]

    near = jnp.stack(joined[:2])
    far = jnp.stack(joined[2:])
    near_crossed = send_y(pick(near, 1 - y, 2))
    far_arrived = [send_x(pick(far, (x + dx) % 4, 1), dx) for dx in (2, 1, 3)]
    near_sum = pick(near, y, 2).astype(F32) + near_crossed.astype(F32)
    far_sum = after(pick(far, x, 1).astype(F32) + sum(a.astype(F32) for a in far_arrived), near_sum)
    near_other = [send_x(pick(near_sum, (x + dx) % 4, 1).astype(BF16), dx) for dx in (2, 1, 3)]
    far_other = send_y(pick(far_sum, 1 - y, 1).astype(BF16))
    near_total = pick(near_sum, x, 1) + sum(a.astype(F32) for a in near_other)
    far_total = pick(far_sum, y, 1) + far_other.astype(F32)
    totals = [near_total[0]] + [
        send_z(value.astype(BF16), dz).astype(F32)
        for dz, value in ((1, near_total[1]), (2, far_total[0]), (3, far_total[1]))
    ]
    joined_sum = jnp.concatenate(totals, 1)

    row = 4 * outs

    def relative_features(value):
        blocks = [lax.dynamic_slice_in_dim(value, (z - dz) % 4 * row, row, value.ndim - 1) for dz in range(4)]
        return jnp.concatenate(blocks, -1)

    loss_scale = float(tokens * lax.axis_size("dp")) ** (-0.5)
    joined_grad, gain_grad = jax.grad(draft_loss, argnums=(0, 1))(
        joined_sum, relative_features(draft_gain), relative_features(cotangent), loss_mask, loss_scale
    )
    gain_full = jnp.zeros_like(gain_grad)
    for dz in range(4):
        gain_full = lax.dynamic_update_slice_in_dim(gain_full, gain_grad[:, dz * row : (dz + 1) * row], (z - dz) % 4 * row, 1)
    joined_grad = joined_grad.astype(BF16)
    blocks = [dz * row + (q ^ dq) * outs for dz in range(4) for dq in range(4)]
    joined_grad = jnp.concatenate([lax.dynamic_slice_in_dim(joined_grad, b, outs, 1) for b in blocks], 1)
    grads = [joined_grad[:, :row]] + [send_z(joined_grad[:, dz * row : (dz + 1) * row], -dz) for dz in (1, 2, 3)]

    def by_x(pieces):
        gathered = jnp.zeros((4, *pieces[0].shape), BF16)
        for dx, piece in enumerate(pieces):
            gathered = lax.dynamic_update_index_in_dim(gathered, piece, (x + dx) % 4, 0)
        return gathered

    near = jnp.concatenate(grads[:2], 0)
    far = jnp.concatenate(grads[2:], 0)
    near_x = [near] + [send_x(near, -dx) for dx in (1, 2, 3)]
    near_own = by_x(near_x)
    near_other = send_y(near_own)
    far_pair = jnp.stack([far, send_y(far)])
    far_all = by_x([far_pair] + [send_x(far_pair, -dx) for dx in (1, 2, 3)])

    grad_gain = after(gain_full, near_x[1])
    for axis, bits in (("dp", (1, 2, 4, 8)), ("tensor", (1, 2, 4))):
        for bit in bits:
            grad_gain = grad_gain + lax.ppermute(grad_gain, axis, [(d, d ^ bit) for d in range(lax.axis_size(axis))])

    def by_y(blocks):
        rows = [jnp.concatenate([low_mids[dz][0], low_mids[dz][1], highs[dz]], 1).reshape(4, 2, part, -1) for dz in blocks]
        return [jnp.stack([pick(r, side, 1) for r in rows], 1) for side in (y, 1 - y)]

    near_features = by_y((0, 1))
    far_features = jnp.stack(by_y((2, 3)), 1)
    terms = [(near_own, near_features[0]), (near_other, near_features[1]), (far_all, far_features)]
    terms = [(left.reshape(-1, row), right.reshape(-1, 3 * width)) for left, right in terms]

    def grad_block(dq):
        columns = slice(dq * outs, (dq + 1) * outs)
        return sum(matmul(left[:, columns], right, (0, 0)) for left, right in terms)

    block3 = send_core(grad_block(3).astype(BF16))
    for_pair = send_pair((grad_block(2).astype(BF16).astype(F32) + block3.astype(F32)).astype(BF16))
    block1 = send_core(grad_block(1).astype(BF16))
    own = grad_block(0).astype(BF16).astype(F32) + block1.astype(F32)
    grad_join = (own + for_pair.astype(F32)).reshape(outs, 3, width)
    return (grad_join, grad_gain)


def solution(mesh):
    return jax.shard_map(
        on_device,
        mesh=mesh,
        in_specs=(
            P("dp", "tensor"),
            P("tensor", None),
            P("tensor", None),
            P("dp", "tensor"),
            P("dp", "tensor"),
            P("dp", "tensor"),
            P("dp", None, "tensor"),
            P(),
            P(None, ("dp", "tensor"), None),
            P(("dp", "tensor")),
        ),
        out_specs=(P("dp", None, "tensor"), P()),
        check_vma=False,
    )
```

```python
import jax
import jax.numpy as jnp
from jax import lax
from jax.experimental import pallas as pl
from jax.experimental.pallas import tpu as pltpu
from jax.sharding import PartitionSpec as P

BLOCK = 128
STEPS = 3
EPS = 1e-05
BF16 = jnp.bfloat16
F32 = jnp.float32


def send_x(value, hops):
    pairs = [(x * 2 + y, ((x + hops) % 4) * 2 + y) for x in range(4) for y in range(2)]
    return lax.ppermute(value, "tensor", pairs)


def send_y(value):
    return lax.ppermute(value, "tensor", [(t, t ^ 1) for t in range(8)])


def send_z(value, hops):
    return lax.ppermute(value, "dp", [(d, (d + 4 * hops) % 16) for d in range(16)])


def send_pair(value):
    return lax.ppermute(value, "dp", [(d, d ^ 2) for d in range(16)])


def send_core(value):
    return lax.ppermute(value, "dp", [(d, d ^ 1) for d in range(16)])


def draft_loss(joined_sum, gain_table, cotangent, token_mask, loss_scale):
    current = joined_sum
    running = jnp.zeros((), F32)
    keeper = token_mask.astype(F32)[:, None]
    for step_index in range(STEPS):
        square_mean = jnp.mean(current * current, axis=-1, keepdims=True)
        normed = current * lax.rsqrt(square_mean + EPS) * gain_table[step_index][None, :]
        current = current + jax.nn.silu(normed)
        running = running + jnp.sum(keeper * cotangent[step_index].astype(F32) * current)
    return running * loss_scale


def project_kernel(places_ref, attention_ref, codes_ref, scales_ref, *refs):
    *first_refs, second_other_ref, second_own_ref, weight_ref = refs
    step = pl.program_id(0)
    place = places_ref[step]
    half, blocks = attention_ref.shape[0] // 2, codes_ref.shape[1] // BLOCK
    for k in range(codes_ref.shape[0] // BLOCK):
        for j in range(blocks):
            at = (slice(k * BLOCK, (k + 1) * BLOCK), slice(j * BLOCK, (j + 1) * BLOCK))
            weight_ref[at] = (codes_ref[at].astype(F32) * scales_ref[k, place * blocks + j]).astype(BF16)
    partial = jnp.dot(attention_ref[...], weight_ref[...], preferred_element_type=F32).astype(BF16)
    for index, first_ref in enumerate(first_refs):

        @pl.when(step // 2 == index)
        def _(first_ref=first_ref):
            first_ref[...] = partial[:half]

    @pl.when(step % 2 == 0)
    def _():
        second_other_ref[...] = partial[half:]

    @pl.when(step % 2 == 1)
    def _():
        second_own_ref[...] = partial[half:]


def project(attention, code_blocks, block_scales, places, width):
    rows, depth = attention.shape
    half, steps = rows // 2, places.shape[0]

    def first_spec(index):
        return pl.BlockSpec((None, half, width), lambda step, places: (jnp.clip(step - 2 * index, 0, 1), 0, 0))

    second_spec = pl.BlockSpec((None, half, width), lambda step, places: (places[step] // 2, 0, 0))
    return pl.pallas_call(
        project_kernel,
        grid_spec=pltpu.PrefetchScalarGridSpec(
            num_scalar_prefetch=1,
            grid=(steps,),
            in_specs=[
                pl.BlockSpec((rows, depth), lambda step, places: (0, 0)),
                pl.BlockSpec((depth, width), lambda step, places: (0, places[step])),
                pl.BlockSpec(memory_space=pltpu.SMEM),
            ],
            out_specs=[first_spec(index) for index in range(steps // 2)] + [second_spec] * 2,
            scratch_shapes=[pltpu.VMEM((depth, width), BF16)],
        ),
        out_shape=[jax.ShapeDtypeStruct((2, half, width), BF16)] * (steps // 2)
        + [jax.ShapeDtypeStruct((steps // 2, half, width), BF16)] * 2,
        compiler_params=pltpu.CompilerParams(vmem_limit_bytes=48 * 2**20),
        cost_estimate=pl.CostEstimate(
            flops=2 * rows * depth * width * steps, bytes_accessed=4 * depth * width * steps, transcendentals=0
        ),
    )(places, attention, code_blocks, block_scales)


def after(value, *others):
    for other in others:
        entry = other[(slice(0, 1),) * other.ndim].reshape(())
        value = value + jnp.minimum(jnp.abs(entry.astype(F32)), 0).astype(value.dtype)
    return value


def matmul(left, right, contract):
    return lax.dot_general(left, right, ((contract[:1], contract[1:]), ((), ())), preferred_element_type=F32)


def on_device(
    attention,
    code_blocks,
    block_scales,
    residual,
    low_feature,
    mid_feature,
    join_weight,
    draft_gain,
    cotangent,
    loss_mask,
):
    dp_index, tensor_index = lax.axis_index("dp"), lax.axis_index("tensor")
    z, q = dp_index // 4, dp_index % 4
    x, y = tensor_index // 2, tensor_index % 2
    tokens, width = residual.shape
    part = tokens // 8
    outs = join_weight.shape[0]

    def pick(value, index, axis):
        return lax.dynamic_index_in_dim(value, index, axis, False)

    low_mid = jnp.stack([low_feature, mid_feature])
    low_mids = {0: low_mid, **{dz: send_z(low_mid, -dz) for dz in (1, 3)}}
    weight = jnp.transpose(join_weight, (1, 0, 2))
    weight_pair = jnp.stack([weight, send_pair(weight)])
    weight_core = send_core(weight_pair)
    weights = jnp.stack([weight_pair, weight_core], 1).reshape(4, *weight.shape)
    weight_all = jnp.concatenate([pick(weights, q ^ i, 0) for i in range(4)], 1)

    half = tokens // 2
    places = jnp.stack([((x + dx) % 4) * 2 + (y ^ dy) for dx in (2, 1, 3, 0) for dy in (1, 0)])
    *to_send, first_own, to_cross, second_own = project(attention, code_blocks, block_scales, places, width)
    crossed = send_y(to_cross)
    to_send = [to_send[0], after(to_send[1], low_mids[1]), after(to_send[2], low_mids[3])]
    low_mids[2] = send_z(after(low_mid, *to_send[1:]), -2)
    arrived = [send_x(value, dx) for dx, value in zip((2, 1, 3), to_send)]
    first = first_own.astype(F32) + sum(a.astype(F32) for a in arrived)
    second = second_own.astype(F32) + crossed.astype(F32)
    first_other = send_y(after(first[0], weight_core).astype(BF16))
    second_other = [send_x(pick(second, (x + dx) % 4, 0).astype(BF16), dx) for dx in (2, 1, 3)]
    residual = residual.astype(F32)
    high_first = residual[:half] + (first[1] + first_other.astype(F32))
    high_second = residual[half:] + (pick(second, x, 0) + sum(a.astype(F32) for a in second_other))
    high = jnp.concatenate([high_first.astype(BF16), high_second.astype(BF16)], 0)

    low_mids = [low_mids[dz] for dz in range(4)]
    early = [jnp.concatenate([value[kind] for value in low_mids], 0) for kind in range(2)]
    early = matmul(early[0], weight_all[0], (1, 1)) + matmul(early[1], weight_all[1], (1, 1))
    early = early.reshape(4, tokens, -1)

    highs = {0: high, 1: send_z(high, -1), 3: send_z(high, -3)}
    highs[2] = send_z(after(high, highs[1]), -2)
    joined = [(early[dz] + matmul(highs[dz], weight_all[2], (1, 1))).astype(BF16) for dz in range(4)]
    joined = [value.reshape(4, 2, part, -1) for value in joined]

    near = jnp.stack(joined[:2])
    far = jnp.stack(joined[2:])
    near_crossed = send_y(pick(near, 1 - y, 2))
    far_arrived = [send_x(pick(far, (x + dx) % 4, 1), dx) for dx in (2, 1, 3)]
    near_sum = pick(near, y, 2).astype(F32) + near_crossed.astype(F32)
    far_sum = after(pick(far, x, 1).astype(F32) + sum(a.astype(F32) for a in far_arrived), near_sum)
    near_other = [send_x(pick(near_sum, (x + dx) % 4, 1).astype(BF16), dx) for dx in (2, 1, 3)]
    far_other = send_y(pick(far_sum, 1 - y, 1).astype(BF16))
    near_total = pick(near_sum, x, 1) + sum(a.astype(F32) for a in near_other)
    far_total = pick(far_sum, y, 1) + far_other.astype(F32)
    totals = [near_total[0]] + [
        send_z(value.astype(BF16), dz).astype(F32)
        for dz, value in ((1, near_total[1]), (2, far_total[0]), (3, far_total[1]))
    ]
    joined_sum = jnp.concatenate(totals, 1)

    row = 4 * outs

    def relative_features(value):
        blocks = [lax.dynamic_slice_in_dim(value, (z - dz) % 4 * row, row, value.ndim - 1) for dz in range(4)]
        return jnp.concatenate(blocks, -1)

    loss_scale = float(tokens * lax.axis_size("dp")) ** (-0.5)
    joined_grad, gain_grad = jax.grad(draft_loss, argnums=(0, 1))(
        joined_sum, relative_features(draft_gain), relative_features(cotangent), loss_mask, loss_scale
    )
    gain_full = jnp.zeros_like(gain_grad)
    for dz in range(4):
        gain_full = lax.dynamic_update_slice_in_dim(gain_full, gain_grad[:, dz * row : (dz + 1) * row], (z - dz) % 4 * row, 1)
    joined_grad = joined_grad.astype(BF16)
    blocks = [dz * row + (q ^ dq) * outs for dz in range(4) for dq in range(4)]
    joined_grad = jnp.concatenate([lax.dynamic_slice_in_dim(joined_grad, b, outs, 1) for b in blocks], 1)
    grads = [joined_grad[:, :row]] + [send_z(joined_grad[:, dz * row : (dz + 1) * row], -dz) for dz in (1, 2, 3)]

    def by_x(pieces):
        gathered = jnp.zeros((4, *pieces[0].shape), BF16)
        for dx, piece in enumerate(pieces):
            gathered = lax.dynamic_update_index_in_dim(gathered, piece, (x + dx) % 4, 0)
        return gathered

    near = jnp.concatenate(grads[:2], 0)
    far = jnp.concatenate(grads[2:], 0)
    near_x = [near] + [send_x(near, -dx) for dx in (1, 2, 3)]
    near_own = by_x(near_x)
    near_other = send_y(near_own)
    far_pair = jnp.stack([far, send_y(far)])
    far_all = by_x([far_pair] + [send_x(far_pair, -dx) for dx in (1, 2, 3)])

    grad_gain = after(gain_full, near_x[1])
    for axis, bits in (("dp", (1, 2, 4, 8)), ("tensor", (1, 2, 4))):
        for bit in bits:
            grad_gain = grad_gain + lax.ppermute(grad_gain, axis, [(d, d ^ bit) for d in range(lax.axis_size(axis))])

    def by_y(blocks):
        rows = [jnp.concatenate([low_mids[dz][0], low_mids[dz][1], highs[dz]], 1).reshape(4, 2, part, -1) for dz in blocks]
        return [jnp.stack([pick(r, side, 1) for r in rows], 1) for side in (y, 1 - y)]

    near_features = by_y((0, 1))
    far_features = jnp.stack(by_y((2, 3)), 1)
    terms = [(near_own, near_features[0]), (near_other, near_features[1]), (far_all, far_features)]
    terms = [(left.reshape(-1, row), right.reshape(-1, 3 * width)) for left, right in terms]

    def grad_block(dq):
        columns = slice(dq * outs, (dq + 1) * outs)
        return sum(matmul(left[:, columns], right, (0, 0)) for left, right in terms)

    block3 = send_core(grad_block(3).astype(BF16))
    for_pair = send_pair((grad_block(2).astype(BF16).astype(F32) + block3.astype(F32)).astype(BF16))
    block1 = send_core(grad_block(1).astype(BF16))
    own = grad_block(0).astype(BF16).astype(F32) + block1.astype(F32)
    grad_join = (own + for_pair.astype(F32)).reshape(outs, 3, width)
    return (grad_join, grad_gain)


def solution(mesh):
    return jax.shard_map(
        on_device,
        mesh=mesh,
        in_specs=(
            P("dp", "tensor"),
            P("tensor", None),
            P("tensor", None),
            P("dp", "tensor"),
            P("dp", "tensor"),
            P("dp", "tensor"),
            P("dp", None, "tensor"),
            P(),
            P(None, ("dp", "tensor"), None),
            P(("dp", "tensor")),
        ),
        out_specs=(P("dp", None, "tensor"), P()),
        check_vma=False,
    )
```
